32 devices in a mesh: gx: 4 (over z), gy: 4 (over x, core), gz: 2 (over y).
Axes of the slice: x: 2, y: 2, z: 4, core: 2. Of those that a mesh axis runs over, the one named last changes fastest.
Arguments:
- velocity: float32 [3, 64, 32, 256], P(None, 'gx', 'gy', 'gz'), may hold values from -6 to 6
- acoustic: float32 [1024, 4, 512], P(('gx', 'gy', 'gz')), may hold values from -6 to 6
- projection: float32 [64, 512], replicated, may hold values from -0.75 to 0.75
- owner_index: int32 [1024, 1], P(('gx', 'gy', 'gz')), may hold values from 0 to 7; in each aligned block of 32 rows (0 to 31, 32 to 63, ...) at most 8 rows name the same one
- slot_element: int32 [32, 64], P(('gx', 'gy', 'gz')), may hold values from 0 to 31
- element_cell: int32 [32, 32], P(('gx', 'gy', 'gz')), may hold values from 0 to 31, each once within a row
Outputs:
- velocity_out: float32 [3, 64, 32, 256], P(None, 'gx', 'gy', 'gz')
- acoustic_out: float32 [1024, 4, 512], P(('gx', 'gy', 'gz'))
The draws below stay inside these ranges and needn't reach their ends.
Inputs may be any that keep to these rules, and one draw needn't show every extreme that they name: `owner_index`: owners are numbered gy index times 2 plus gz index within the sender's gx plane; among one device's 32 rows no owner appears more than 8 times. Slot q of a device feeds its stored element slot_element[q]. `element_cell`: each row is a permutation of the brick cells of one device.
All inputs are finite; a program needn't handle non-finite values.
Results may differ from the reference program's by a relative error of at most 0.0019.
Values may be sent and summed in bfloat16 or wider, within the bound.
A program may use at most 128 MiB of HBM per device.

```python
import math
import jax
import jax.numpy as jnp
import numpy as np
from jax import lax

CX = 16
CY = 8
CZ = 128
VS = 4
ORDER = 7
EBX = 1
EBY = 2
EBZ = 16
NODES = 512
VOL = 64
NV = 32
ELEM = 32
PEERS = 8
CAP = 8
SLOTS = 64
NX = 64
NY = 32
NZ = 256
ELEMENTS = 1024
N_GX = 4
N_GY = 4
N_GZ = 2
DEVICES = 32


def with_ends(result, rng, least, largest):
    longest = result.shape.index(max(result.shape))
    spots = []
    for shift in (0, 1):
        where = [jax.random.randint(jax.random.fold_in(rng, axis), (), 0, length) for axis, length in enumerate(result.shape)]
        where[longest] = (where[longest] + shift) % result.shape[longest]
        spots.append(tuple(where))
    return result.at[spots[0]].set(least).at[spots[1]].set(largest)


def block_scale(rng, shape, cuts, least, high):
    def one(axis_at, blocks):
        draws = jax.random.uniform(jax.random.fold_in(jax.random.fold_in(rng, 6), axis_at), (blocks,), jnp.float32, least / len(cuts), high / len(cuts))
        return jnp.repeat(jnp.exp(draws), shape[axis_at] // blocks).reshape((-1,) + (1,) * (len(shape) - axis_at - 1))

    gain = one(*cuts[0])
    for cut in cuts[1:]:
        gain = gain * one(*cut)
    return gain


def assign_block(rng, own, number, rows, amount, top, most, skew):
    sequence = jax.random.permutation(rng, amount)
    packed, ordinary = portions_of(amount, rows * top, most, skew, True), portions_of(amount, rows * top, most, skew, False)
    places = jnp.arange(amount)

    def named(sizes, rotation):
        used = int((sizes > 0).sum())
        fixed = max(1, used // 4)
        moved = fixed + (places - fixed + rotation * (used - fixed)) % max(1, amount - fixed)
        return jnp.zeros((amount,), jnp.int32).at[sequence[jnp.where(places < fixed, places, moved)]].set(jnp.asarray(sizes, jnp.int32))

    sizes = jnp.where(number % 4 == 0, named(packed, number // 4), named(ordinary, number - number // 4 - 1))
    mixed = jax.random.permutation(jax.random.fold_in(own, 3), amount)
    giver, sink = mixed[0:amount // 2 * 2:2], mixed[1:amount // 2 * 2:2]
    slack = jnp.minimum(sizes[giver] - 1, most - sizes[sink]) // 2
    slack = jnp.where((giver == sequence[0]) | (sink == sequence[0]) | (sizes[sink] == 0), 0, jnp.maximum(slack, 0))
    moved = jax.random.randint(jax.random.fold_in(own, 4), (amount // 2,), 0, 1 << 20) % (slack + 1)
    sizes = sizes.at[giver].add(-moved).at[sink].add(moved)
    members = jnp.searchsorted(jnp.cumsum(sizes), jnp.arange(rows * top), side="right").astype(jnp.int32)
    listing = members.reshape(top, rows).T
    listing = listing[jax.random.permutation(jax.random.fold_in(own, 1), rows)]
    rotation = jax.random.randint(jax.random.fold_in(own, 2), (rows, 1), 0, top)
    return jnp.take_along_axis(listing, (jnp.arange(top)[None, :] + rotation) % top, axis=1)


def portions_of(count, total, limit, slope, full):
    portions = [(1 << 20) // math.isqrt(rank ** slope) + 1 for rank in range(1, count + 1)]
    largest = limit if full else min(limit, max(-(-total // count), total * portions[0] // sum(portions)))
    least = 1 if total - largest >= count - 1 else 0
    given, surplus = [largest] + [least] * (count - 1), total - largest - least * (count - 1)
    while surplus > 0:
        movable = [i for i in range(1, count) if given[i] < largest] or [i for i in range(1, count) if given[i] < limit]
        pool, budget = sum([portions[i] for i in movable]), surplus
        for i in movable:
            more = min(limit - given[i], max(1, budget * portions[i] // pool), surplus)
            given[i] = given[i] + more
            surplus = surplus - more
    return np.array(given)


def noise(rng, dims, scale, most, cuts=(), held_as=jnp.bfloat16):
    level = block_scale(rng, dims, cuts, -0.22, 0.18) if cuts else 1.0
    array = jax.random.normal(rng, dims, jnp.float32) * scale * level
    return jnp.minimum(jnp.maximum(array, -most), most).astype(held_as)


def setup_inputs(seed: int = 0) -> dict:
    seeds = jax.random.split(jax.random.key(seed), 7)
    velocity = noise(seeds[0], (3, NX, NY, NZ), 1.0, 6.0, ((1, 4), (2, 4), (3, 2)), jnp.float32)
    acoustic = noise(seeds[1], (ELEMENTS, 4, NODES), 1.0, 6.0, ((0, 32),), jnp.float32)
    projection = noise(seeds[2], (VOL, NODES), VOL ** -0.5, 0.75, (), jnp.float32)
    owner_index_keys = jax.random.split(jax.random.fold_in(seeds[3], 1), (DEVICES * NV) // NV)
    owner_index_turns = jax.random.permutation(jax.random.fold_in(seeds[3], 3), (DEVICES * NV) // NV)
    owner_index = jax.vmap(lambda own, number: assign_block(jax.random.fold_in(seeds[3], 2), own, number, NV, N_GY * N_GZ, 1, CAP, 2))(owner_index_keys, owner_index_turns).reshape((DEVICES * NV, 1))
    slot_element = with_ends(jax.random.randint(seeds[4], (DEVICES, N_GY * N_GZ * CAP), 0, ELEM), jax.random.fold_in(seeds[4], 1), 0, ELEM - 1).astype(jnp.int32)
    element_cell = jax.vmap(lambda own: jax.random.permutation(own, ELEM))(jax.random.split(seeds[5], DEVICES)).reshape((DEVICES, ELEM)).astype(jnp.int32)
    return {"velocity": velocity, "acoustic": acoustic, "projection": projection, "owner_index": owner_index, "slot_element": slot_element, "element_cell": element_cell}


HIGHEST = lax.Precision.HIGHEST
FLOW_STEP = 0.1
VISCOSITY = 0.05
WAVE_STEP = 0.02
SOURCE_GAIN = 25.0


def legendre_table(points, order):
    columns = [points * 0.0 + 1.0, points]
    for degree in range(2, order + 1):
        columns.append(((2 * degree - 1) * points * columns[degree - 1] - (degree - 1) * columns[degree - 2]) / degree)
    return np.stack(columns, axis=1)


def lobatto_tables(order):
    point_count = order + 1
    points = -np.cos(np.pi * np.arange(point_count) / order)
    for newton_step in range(60):
        legendre = legendre_table(points, order)
        points = points - (points * legendre[:, order] - legendre[:, order - 1]) / (point_count * legendre[:, order])
    legendre = legendre_table(points, order)
    highest = legendre[:, order]
    spacing = points[:, None] - points[None, :] + np.eye(point_count)
    derivative = highest[:, None] / (highest[None, :] * spacing)
    derivative = derivative * (1.0 - np.eye(point_count))
    derivative[0, 0] = -order * point_count / 4.0
    derivative[order, order] = order * point_count / 4.0
    return derivative


def wave_tables(order):
    width = order + 1
    derivative = lobatto_tables(order)
    unit = np.eye(width)
    along_x = np.kron(np.kron(derivative, unit), unit)
    along_y = np.kron(np.kron(unit, derivative), unit)
    along_z = np.kron(np.kron(unit, unit), derivative)
    gradient_table = np.concatenate([along_x.T, along_y.T, along_z.T], axis=1)
    divergence_table = np.concatenate([along_x.T, along_y.T, along_z.T], axis=0)
    selector = np.zeros((width ** 3, 6 * width * width))
    for face_id in range(6):
        along = face_id // 2
        level = (width - 1) * (face_id % 2)
        for first in range(width):
            for second in range(width):
                index_list = [first, second]
                index_list.insert(along, level)
                node_id = (index_list[0] * width + index_list[1]) * width + index_list[2]
                selector[node_id, face_id * width * width + first * width + second] = 1.0
    lift_scale = order * (order + 1) / 2.0
    return (jnp.asarray(gradient_table, jnp.float32), jnp.asarray(divergence_table, jnp.float32), jnp.asarray(selector, jnp.float32), lift_scale)


def shifted(padded, along):
    lower_index = [slice(None), slice(1, -1), slice(1, -1), slice(1, -1)]
    upper_index = list(lower_index)
    lower_index[along + 1] = slice(0, -2)
    upper_index[along + 1] = slice(2, None)
    return padded[tuple(lower_index)], padded[tuple(upper_index)]


def advance(padded):
    centre = padded[:, 1:-1, 1:-1, 1:-1]
    rates = jnp.zeros_like(centre)
    slopes = []
    for along in range(3):
        lower_cells, upper_cells = shifted(padded, along)
        gradient_part = 0.5 * (upper_cells - lower_cells)
        slopes.append(gradient_part)
        rates = rates - centre[along] * gradient_part + VISCOSITY * (upper_cells + lower_cells - 2.0 * centre)
    updated = centre + FLOW_STEP * rates
    swirl = jnp.stack([slopes[1][2] - slopes[2][1], slopes[2][0] - slopes[0][2], slopes[0][1] - slopes[1][0]])
    lamb_vector = jnp.stack([swirl[1] * centre[2] - swirl[2] * centre[1], swirl[2] * centre[0] - swirl[0] * centre[2], swirl[0] * centre[1] - swirl[1] * centre[0]])
    return updated, lamb_vector


def face_terms(jumps, lift_scale):
    pieces = []
    for face_id in range(6):
        along = face_id // 2
        normal = 1.0 if face_id % 2 else -1.0
        face_jump = jumps[..., face_id, :]
        pressure_jump = face_jump[..., 0, :]
        normal_jump = face_jump[..., 1 + along, :]
        flux_rows = []
        for variable in range(4):
            if variable == 0:
                flux_rows.append(normal * normal_jump)
            elif variable == 1 + along:
                flux_rows.append(normal * pressure_jump)
            else:
                flux_rows.append(jnp.zeros_like(pressure_jump))
        face_flux = jnp.stack(flux_rows, axis=-2)
        pieces.append(0.5 * lift_scale * (face_flux - face_jump))
    return jnp.stack(pieces, axis=-2)


def outer_traces(padded):
    extent = [padded.shape[0] - 2, padded.shape[1] - 2, padded.shape[2] - 2]
    pieces = []
    for face_id in range(6):
        along = face_id // 2
        offset = [1, 1, 1]
        offset[along] = 2 if face_id % 2 else 0
        neighbour_block = padded[offset[0]:offset[0] + extent[0], offset[1]:offset[1] + extent[1], offset[2]:offset[2] + extent[2]]
        pieces.append(neighbour_block[..., face_id ^ 1, :])
    return jnp.stack(pieces, axis=-2)


def face_values(wave_state, selector):
    elements, variables, points = wave_state.shape
    return jnp.dot(wave_state.reshape(elements * variables, points), selector, precision=HIGHEST).reshape(elements, variables, 6, -1)


def wave_update(wave_state, inner_trace, outer_trace, source, tables):
    gradient_table, divergence_table, selector, lift_scale = tables
    elements, variables, points = wave_state.shape
    gradient = jnp.dot(wave_state[:, 0], gradient_table, precision=HIGHEST).reshape(elements, 3, points)
    divergence = jnp.dot(wave_state[:, 1:].reshape(elements, 3 * points), divergence_table, precision=HIGHEST)
    corrections = face_terms(inner_trace - outer_trace, lift_scale).reshape(elements * variables, -1)
    lifted = jnp.dot(corrections, selector.T, precision=HIGHEST).reshape(elements, variables, points)
    rates = jnp.concatenate([-divergence[:, None], -gradient - SOURCE_GAIN * source], axis=1) + lifted
    return wave_state + WAVE_STEP * rates


def to_global_brick(stored, element_cell):
    device_rows = jnp.arange(DEVICES, dtype=jnp.int32)[:, None]
    local_brick = jnp.zeros_like(stored).at[device_rows, element_cell].set(stored)
    trailing = stored.shape[2:]
    shaped = local_brick.reshape((N_GX, N_GY, N_GZ, EBX, EBY, EBZ) + trailing)
    extra = tuple(range(6, 6 + len(trailing)))
    return shaped.transpose((0, 3, 1, 4, 2, 5) + extra).reshape((N_GX * EBX, N_GY * EBY, N_GZ * EBZ) + trailing)


def from_global_brick(brick, element_cell):
    trailing = brick.shape[3:]
    shaped = brick.reshape((N_GX, EBX, N_GY, EBY, N_GZ, EBZ) + trailing)
    extra = tuple(range(6, 6 + len(trailing)))
    local_brick = shaped.transpose((0, 2, 4, 1, 3, 5) + extra).reshape((DEVICES, ELEM) + trailing)
    device_rows = jnp.arange(DEVICES, dtype=jnp.int32)[:, None]
    return local_brick[device_rows, element_cell]


def global_sources(lamb_vector, projection, owner_index, slot_element, element_cell):
    coarse = lamb_vector.reshape(3, NX // 2, 2, NY // 2, 2, NZ // 2, 2).mean(axis=(2, 4, 6))
    blocks = coarse.reshape(3, N_GX, CX // (2 * VS), VS, N_GY, CY // (2 * VS), VS, N_GZ, CZ // (2 * VS), VS)
    volumes = blocks.transpose(1, 4, 7, 2, 5, 8, 0, 3, 6, 9).reshape(DEVICES, NV, 3 * VOL).astype(jnp.bfloat16)
    owners = owner_index.reshape(DEVICES, NV).astype(jnp.int32)
    order_index = jnp.arange(NV, dtype=jnp.int32)
    matches = (owners[:, :, None] == owners[:, None, :]) & (order_index[None, None, :] < order_index[None, :, None])
    ranking = jnp.sum(matches.astype(jnp.int32), axis=-1).astype(jnp.int32)
    slots = owners * CAP + ranking
    placement = (slots[:, None, :] == jnp.arange(SLOTS, dtype=jnp.int32)[None, :, None]).astype(jnp.float32)
    sent = jnp.einsum("dsv,dvc->dsc", placement, volumes.astype(jnp.float32), precision=HIGHEST).astype(jnp.bfloat16)
    received = sent.reshape(N_GX, PEERS, PEERS, CAP, 3 * VOL).transpose(0, 2, 1, 3, 4).reshape(DEVICES, SLOTS, 3, VOL)
    projected = jnp.dot(received.astype(jnp.float32).reshape(-1, VOL), projection, precision=HIGHEST).reshape(DEVICES, SLOTS, 3 * NODES)
    target = (slot_element[:, None, :] == jnp.arange(ELEM, dtype=jnp.int32)[None, :, None]).astype(jnp.float32)
    source = jnp.einsum("dep,dpc->dec", target, projected, precision=HIGHEST).reshape(DEVICES, ELEM, 3, NODES)
    return to_global_brick(source, element_cell)


def reference(velocity, acoustic, projection, owner_index, slot_element, element_cell):
    tables = wave_tables(ORDER)
    selector = tables[2]
    wave_state = to_global_brick(acoustic.reshape(DEVICES, ELEM, 4, NODES), element_cell)
    brick_shape = wave_state.shape
    flow = velocity
    for time_step in range(2):
        padded = jnp.pad(flow, ((0, 0), (1, 1), (1, 1), (1, 1)), mode="wrap")
        flow, lamb_vector = advance(padded)
        source = global_sources(lamb_vector, projection, owner_index, slot_element, element_cell)
        flat_state = wave_state.reshape(-1, 4, NODES)
        inner_trace = face_values(flat_state, selector)
        inner_brick = inner_trace.reshape(brick_shape[:3] + (4, 6, -1))
        padded_trace = jnp.pad(inner_brick, ((1, 1), (1, 1), (1, 1), (0, 0), (0, 0), (0, 0)), mode="wrap")
        outer_trace = outer_traces(padded_trace).reshape(inner_trace.shape)
        flat_state = wave_update(flat_state, inner_trace, outer_trace, source.reshape(-1, 3, NODES), tables)
        wave_state = flat_state.reshape(brick_shape)
    acoustic_out = from_global_brick(wave_state, element_cell).reshape(ELEMENTS, 4, NODES)
    return flow, acoustic_out
```

```python
import functools

import jax
import jax.numpy as jnp
import numpy as np
from jax import lax
from jax.experimental import pallas as pl
from jax.experimental.pallas import tpu as pltpu
from jax.sharding import PartitionSpec as P

VS = 4
ORDER = 7
EBX = 1
EBY = 2
EBZ = 16
K = ORDER + 1
FACE = K * K
NODES = K**3

HIGHEST = lax.Precision.HIGHEST
FLOW_STEP = 0.1
VISCOSITY = 0.05
WAVE_STEP = 0.02
SOURCE_GAIN = 25.0
MESH = pl.DeviceIdType.MESH


def legendre_table(points, order):
    columns = [points * 0.0 + 1.0, points]
    for degree in range(2, order + 1):
        columns.append(
            ((2 * degree - 1) * points * columns[degree - 1] - (degree - 1) * columns[degree - 2])
            / degree
        )
    return np.stack(columns, axis=1)


def lobatto_tables(order):
    point_count = order + 1
    points = -np.cos(np.pi * np.arange(point_count) / order)
    for newton_step in range(60):
        legendre = legendre_table(points, order)
        points = points - (points * legendre[:, order] - legendre[:, order - 1]) / (
            point_count * legendre[:, order]
        )
    legendre = legendre_table(points, order)
    highest = legendre[:, order]
    spacing = points[:, None] - points[None, :] + np.eye(point_count)
    derivative = highest[:, None] / (highest[None, :] * spacing)
    derivative = derivative * (1.0 - np.eye(point_count))
    derivative[0, 0] = -order * point_count / 4.0
    derivative[order, order] = order * point_count / 4.0
    return derivative


def iota(shape, axis):
    return lax.broadcasted_iota(jnp.int32, shape, axis)


def as_float(mask):
    return jnp.where(mask, 1.0, 0.0).astype(jnp.float32)


def to_column(row, count):
    eye = iota((count, count), 0) == iota((count, count), 1)
    return jnp.sum(jnp.where(eye, row, 0.0), axis=1, keepdims=True)


def to_row(column, count):
    eye = iota((count, count), 0) == iota((count, count), 1)
    return jnp.sum(jnp.where(eye, column, 0.0), axis=0, keepdims=True)


def spread_row(column, count, width, group):
    pick = iota((count, width), 0) == iota((count, width), 1) // group
    return jnp.sum(jnp.where(pick, column, 0.0), axis=0, keepdims=True)


def split(value):
    high = value.astype(jnp.bfloat16)
    low = (value - high.astype(jnp.float32)).astype(jnp.bfloat16)
    return high, low


def dot(a, b, contract=((1,), (0,)), precision=None):
    return lax.dot_general(
        a, b, (contract, ((), ())), preferred_element_type=jnp.float32, precision=precision
    )


def swap(value, group, along, width):
    axis = value.ndim - 1
    total = 4 * width
    here = (1 + along) * width
    up = pltpu.roll(value, here, axis)
    down = up if 2 * here == total else pltpu.roll(value, total - here, axis)
    return jnp.where(group == 0, down, jnp.where(group == 1 + along, up, 0.0))


def derive(values, table):
    half = K // 2
    even = [values[j] + values[K - 1 - j] for j in range(half)]
    odd = [values[j] - values[K - 1 - j] for j in range(half)]
    result = [None] * K
    for a in range(half):
        first = sum(
            float(0.5 * (table[a, j] - table[a, K - 1 - j])) * odd[j] for j in range(half)
        )
        second = sum(
            float(0.5 * (table[a, j] + table[a, K - 1 - j])) * even[j] for j in range(half)
        )
        result[a] = first + second
        result[K - 1 - a] = first - second
    return result


def kernel(
    sizes,
    u_in, ac_in, proj_in, owner_in, slot_in, cell_in,
    u_out, ac_out,
    flow, y_send, y_recv, z_send, z_recv, tr_send, tr_recv, vol_send, vol_recv,
    q_ref, acc, lhs, place, gather, proj_ref,
    v_ssem, v_rsem, t_ssem, t_rsem, p_ssem, p_rsem,
):
    nx, ny, nz, X, Y, Z, E, NV, cap = sizes
    peers = ny * nz
    gx, gy, gz = lax.axis_index("gx"), lax.axis_index("gy"), lax.axis_index("gz")
    me = gy * nz + gz
    across = [
        {"gx": lax.rem(gx + nx - 1, nx)}, {"gx": lax.rem(gx + 1, nx)},
        {"gy": lax.rem(gy + ny - 1, ny)}, {"gy": lax.rem(gy + 1, ny)},
        {"gz": lax.rem(gz + nz - 1, nz)}, {"gz": lax.rem(gz + 1, nz)},
    ]
    others = []
    for k in range(1, peers):
        p = lax.rem(me + k, peers)
        others.append((p, {"gy": lax.div(p, nz), "gz": lax.rem(p, nz)}))

    barrier = pltpu.get_barrier_semaphore()
    for target in across[:2] + [t for _, t in others]:
        pl.semaphore_signal(barrier, inc=1, device_id=target, device_id_type=MESH)

    lane = iota((Y, Z), 1)
    sub = iota((Y, Z), 0)

    def pack(t, x, values, carry):
        low, high = carry
        for c in range(3):
            at = c * X + x
            low = jnp.where(lane == at, pltpu.roll(values[c], at, 1), low)
            high = jnp.where(lane == at, pltpu.roll(values[c], at + 1, 1), high)
            y_send[t, 0, c, pl.ds(x, 1), :] = values[c][0:1]
            y_send[t, 1, c, pl.ds(x, 1), :] = values[c][Y - 1:Y]
        return low, high

    def fill(x, carry):
        values = [u_in[c, x] for c in range(3)]
        for c in range(3):
            flow[0, c, x + 1] = values[c]
        return pack(0, x, values, carry)

    blank = jnp.zeros((Y, Z), jnp.float32)

    def velocity_copies(t):
        result = []
        for f in range(6):
            s = f % 2
            if f < 2:
                src = flow.at[t, :, X if s else 1]
                dst = flow.at[t, :, 0 if s else X + 1]
            elif f < 4:
                src, dst = y_send.at[t, s], y_recv.at[t, 1 - s]
            else:
                src, dst = z_send.at[t, s], z_recv.at[t, 1 - s]
            result.append(
                pltpu.make_async_remote_copy(
                    src_ref=src, dst_ref=dst, send_sem=v_ssem.at[t, f],
                    recv_sem=v_rsem.at[t, f ^ 1], device_id=across[f], device_id_type=MESH,
                )
            )
        return result

    def trace_copies(t):
        return [
            pltpu.make_async_remote_copy(
                src_ref=tr_send.at[t, f], dst_ref=tr_recv.at[t, f ^ 1],
                send_sem=t_ssem.at[t, f], recv_sem=t_rsem.at[t, f ^ 1],
                device_id=across[f], device_id_type=MESH,
            )
            for f in range(6)
        ]

    def volume_copies(t):
        return [
            pltpu.make_async_remote_copy(
                src_ref=vol_send.at[t, p], dst_ref=vol_recv.at[t, me],
                send_sem=p_ssem.at[t, k], recv_sem=p_rsem.at[t, k],
                device_id=target, device_id_type=MESH,
            )
            for k, (p, target) in enumerate(others)
        ]

    low, high = lax.fori_loop(0, X, fill, (blank, blank))
    z_send[0, 0] = low
    z_send[0, 1] = high
    pl.semaphore_wait(barrier, peers + 1)
    v0 = velocity_copies(0)
    for f in (0, 1, 4, 5, 2, 3):
        v0[f].start()

    L4 = 4 * E
    cell_row = cell_in[...].astype(jnp.float32)
    rows = iota((L4, E), 0)
    cell_rep = jnp.sum(
        jnp.where(iota((L4, E), 1) == rows // 4, cell_row, 0.0), axis=1, keepdims=True
    )
    r = iota((L4, L4), 0)
    l = iota((L4, L4), 1)
    perm = as_float(
        l.astype(jnp.float32) == ((r % 4) * E).astype(jnp.float32) + cell_rep
    ).astype(jnp.bfloat16)
    ah, al = split(ac_in[...].T)
    q_ref[...] = dot(
        jnp.concatenate([ah, al], axis=1), jnp.concatenate([perm, perm], axis=0)
    )

    def trace(f):
        a, s = f // 2, f % 2
        if a == 0:
            return q_ref[s * (K - 1) * FACE:s * (K - 1) * FACE + FACE, :]
        if a == 1:
            base = s * (K - 1) * K
            return jnp.concatenate(
                [q_ref[i * FACE + base:i * FACE + base + K, :] for i in range(K)], axis=0
            )
        return q_ref[pl.ds(s * (K - 1), FACE, stride=K), :]

    def send_traces(t):
        for f in range(6):
            tr_send[t, f] = trace(f).astype(jnp.bfloat16)
        copies = trace_copies(t)
        for copy in copies:
            copy.start()
        return copies

    t0 = send_traces(0)

    cells = VS**3
    own = owner_in[...].astype(jnp.float32)
    own_row = to_row(own, NV)
    matches = (own == own_row) & (iota((NV, NV), 1) < iota((NV, NV), 0))
    rank = jnp.sum(as_float(matches), axis=1, keepdims=True)
    slot_of = own * float(cap) + rank
    W = NV * 2 * VS
    R = peers * cap * VS
    slot_row = spread_row(slot_of, NV, W, 2 * VS)
    wl = iota((1, W), 1)
    goal = slot_row * float(VS) + ((wl % (2 * VS)) // 2).astype(jnp.float32)
    goal = jnp.where(wl % 2 == 0, goal, -1.0)
    place[...] = as_float(iota((R, W), 0).astype(jnp.float32) == goal).astype(jnp.bfloat16)

    slots = peers * cap
    slot_col = to_column(slot_in[...].astype(jnp.float32), slots)
    element_row = spread_row(slot_col, slots, R, VS)
    cell_col = to_column(cell_row, E)
    target_row = jnp.sum(
        jnp.where(iota((E, R), 0).astype(jnp.float32) == element_row, cell_col, 0.0),
        axis=0, keepdims=True,
    )
    goal = target_row + ((iota((1, R), 1) % VS) * E).astype(jnp.float32)
    gather[...] = as_float(iota((VS * E, R), 0).astype(jnp.float32) == goal).astype(jnp.bfloat16)

    PB = VS * Y
    pr = iota((VS * PB, cells), 0)
    pc = iota((VS * PB, cells), 1)
    source_cell = ((pr % PB) // Y * VS + (pr % Y) // 2) * VS + pr // PB
    select = as_float((source_cell == pc) & (pr % 2 == 0)) * (-WAVE_STEP * SOURCE_GAIN)
    arranged = dot(select, proj_in[...], precision=HIGHEST).T
    ph, plo = split(arranged)
    proj_ref[:, :VS * PB] = ph
    proj_ref[:, VS * PB:] = plo

    table = -WAVE_STEP * lobatto_tables(ORDER)
    group3 = iota((K, K, L4), 2) // E
    group2 = iota((FACE, L4), 1) // E
    sub3 = iota((K, K, L4), 1)

    def local_rates():
        factors = []
        subl = iota((K, L4), 0)
        for k in range(K):
            factor = jnp.zeros((K, L4), jnp.float32)
            for c in range(K):
                factor = jnp.where(subl == c, float(table[c, (c - k) % K]), factor)
            factors.append(factor)

        def first(i, carry):
            at = pl.multiple_of(i * FACE, FACE)
            x = q_ref[pl.ds(at, FACE), :].reshape(K, K, L4)
            total = x
            s2 = swap(x, group3, 2, E)
            for k in range(K):
                rolled = s2 if k == 0 else pltpu.roll(s2, k, 1)
                total = total + factors[k][None] * rolled
            s1 = swap(x, group3, 1, E)
            parts = derive([s1[j] for j in range(K)], table)
            total = total + jnp.stack(parts)
            acc[pl.ds(at, FACE), :] = total.reshape(FACE, L4)
            return carry

        lax.fori_loop(0, K, first, 0)

        def second(i, carry):
            ats = [pl.multiple_of(a * FACE + i * K, K) for a in range(K)]
            x = jnp.stack([q_ref[pl.ds(at, K), :] for at in ats])
            s0 = swap(x, group3, 0, E)
            parts = derive([s0[j] for j in range(K)], table)
            for at, part in zip(ats, parts):
                acc[pl.ds(at, K), :] += part
            return carry

        lax.fori_loop(0, K, second, 0)

    lane2 = iota((FACE, L4), 1)
    y_of = (lane2 % E) // EBZ
    z_of = lane2 % EBZ
    scale = WAVE_STEP * 0.5 * ORDER * (ORDER + 1) / 2.0

    def add_flux(t):
        for f in range(6):
            a, s = f // 2, f % 2
            inner = trace(f)
            other = tr_recv[t, f].astype(jnp.float32)
            if a == 0:
                outer = other
            elif a == 1:
                mine = trace(f ^ 1)
                edge = 0 if s else EBY - 1
                mixed = jnp.where(y_of == edge, other, mine)
                near = EBZ if s == 0 else L4 - EBZ
                wrap = (L4 - (EBY - 1) * EBZ) if s == 0 else (EBY - 1) * EBZ
                outer = jnp.where(
                    y_of == (EBY - 1 if s else 0),
                    pltpu.roll(mixed, wrap, 1), pltpu.roll(mixed, near, 1),
                )
            else:
                mine = trace(f ^ 1)
                edge = 0 if s else EBZ - 1
                mixed = jnp.where(z_of == edge, other, mine)
                near = 1 if s == 0 else L4 - 1
                wrap = (L4 - (EBZ - 1)) if s == 0 else EBZ - 1
                outer = jnp.where(
                    z_of == (EBZ - 1 if s else 0),
                    pltpu.roll(mixed, wrap, 1), pltpu.roll(mixed, near, 1),
                )
            jump = inner - outer
            turned = swap(jump, group2, a, E)
            flux = scale * ((turned if s else -turned) - jump)
            if a == 0:
                base = s * (K - 1) * FACE
                acc[base:base + FACE, :] += flux
            elif a == 1:
                base = s * (K - 1) * K
                for i in range(K):
                    at = i * FACE + base
                    acc[at:at + K, :] += flux[i * K:(i + 1) * K]
            else:
                where = pl.ds(s * (K - 1), FACE, stride=K)
                acc[where, :] = acc[where, :] + flux

    def flow_step(t):
        z_low = z_recv[t, 0]
        z_high = z_recv[t, 1]

        def column(x, carry):
            centre = [flow[t, c, x + 1] for c in range(3)]
            below, above = [], []
            for c in range(3):
                at = c * X + x
                u = centre[c]
                pair = (flow[t, c, x], flow[t, c, x + 2])
                y_low = y_recv[t, 0, c, pl.ds(x, 1), :]
                y_high = y_recv[t, 1, c, pl.ds(x, 1), :]
                ym = jnp.where(sub == 0, y_low, pltpu.roll(u, 1, 0))
                yp = jnp.where(sub == Y - 1, y_high, pltpu.roll(u, Y - 1, 0))
                zm = jnp.where(
                    lane == 0, pltpu.roll(z_low, lax.rem(Z - at, Z), 1), pltpu.roll(u, 1, 1)
                )
                zp = jnp.where(
                    lane == Z - 1, pltpu.roll(z_high, Z - 1 - at, 1), pltpu.roll(u, Z - 1, 1)
                )
                below.append((pair[0], ym, zm))
                above.append((pair[1], yp, zp))
            slope = [[0.5 * (above[c][a] - below[c][a]) for c in range(3)] for a in range(3)]
            updated = []
            for c in range(3):
                rate = VISCOSITY * (
                    (above[c][0] + below[c][0])
                    + (above[c][1] + below[c][1])
                    + (above[c][2] + below[c][2])
                    - 6.0 * centre[c]
                )
                for a in range(3):
                    rate = rate - centre[a] * slope[a][c]
                updated.append(centre[c] + FLOW_STEP * rate)
            w = [
                slope[1][2] - slope[2][1], slope[2][0] - slope[0][2], slope[0][1] - slope[1][0]
            ]
            lamb = [
                w[1] * centre[2] - w[2] * centre[1],
                w[2] * centre[0] - w[0] * centre[2],
                w[0] * centre[1] - w[1] * centre[0],
            ]
            if t == 0:
                for c in range(3):
                    flow[1, c, x + 1] = updated[c]
                carry = pack(1, x, updated, carry)
            else:
                for c in range(3):
                    u_out[c, x] = updated[c]
            return lamb, carry

        def couple(i, carry):
            first, carry = column(2 * i, carry)
            second, carry = column(2 * i + 1, carry)
            block = lax.div(i, VS)
            row = lax.rem(i, VS)
            for c in range(3):
                total = first[c] + second[c]
                total = total + pltpu.roll(total, Y - 1, 0)
                total = total + pltpu.roll(total, Z - 1, 1)
                at = pl.multiple_of(c * PB + row * Y, Y)
                lhs[block, pl.ds(at, Y), :] = 0.125 * total
            return carry

        carry = lax.fori_loop(0, X // 2, couple, (blank, blank))
        if t == 0:
            z_send[1, 0] = carry[0]
            z_send[1, 1] = carry[1]

    def send_volumes(t):
        wide = jnp.concatenate([lhs[i] for i in range(X // (2 * VS))], axis=1)
        sent = dot(place[...], wide.astype(jnp.bfloat16), ((1,), (1,)))
        vol_send[t] = sent.astype(vol_send.dtype).reshape(peers, cap * VS, 4 * PB)
        copies = volume_copies(t)
        for copy in copies:
            copy.start()
        vol_recv[t, me] = vol_send[t, me]
        return copies

    def add_source(t):
        received = vol_recv[t].reshape(R, 4 * PB).astype(jnp.bfloat16)
        summed = dot(gather[...], received).T
        group = iota((PB, L4), 1) // E
        blocks = []
        for c in range(VS):
            block = jnp.zeros((PB, L4), jnp.float32)
            for v in range(3):
                part = summed[v * PB:(v + 1) * PB]
                shift = ((1 + v - c) * E) % L4
                if shift:
                    part = pltpu.roll(part, shift, 1)
                block = jnp.where(group == 1 + v, part, block)
            blocks.append(block)
        bh, bl = split(jnp.concatenate(blocks, axis=0))
        source = dot(proj_ref[...], jnp.concatenate([bh, bh], axis=0))
        source = source + dot(proj_ref[:, :VS * PB], bl)
        return acc[...] + source

    lhs[...] = jnp.zeros_like(lhs)
    local_rates()
    for copy in v0:
        copy.wait_recv()
    flow_step(0)
    p0 = send_volumes(0)
    v1 = velocity_copies(1)
    for f in (0, 1, 4, 5, 2, 3):
        v1[f].start()
    for copy in t0:
        copy.wait_recv()
    add_flux(0)
    for copy in v1:
        copy.wait_recv()
    flow_step(1)
    p1 = send_volumes(1)
    for copy in p0:
        copy.wait_recv()
    q_ref[...] = add_source(0)
    t1 = send_traces(1)
    local_rates()
    for copy in t1:
        copy.wait_recv()
    add_flux(1)
    for copy in p1:
        copy.wait_recv()
    final = add_source(1)
    fh, fl = split(final)
    ac_out[...] = dot(
        jnp.concatenate([perm, perm], axis=1), jnp.concatenate([fh, fl], axis=1), ((1,), (1,))
    )
    for copies in (v0, t0, p0, v1, t1, p1):
        for copy in copies:
            copy.wait_send()


def on_device(velocity, acoustic, projection, owner_index, slot_element, element_cell):
    nx, ny, nz = lax.axis_size("gx"), lax.axis_size("gy"), lax.axis_size("gz")
    _, X, Y, Z = velocity.shape
    E = acoustic.shape[0]
    NV = owner_index.shape[0]
    peers = ny * nz
    cap = slot_element.shape[1] // peers
    sizes = (nx, ny, nz, X, Y, Z, E, NV, cap)
    R = peers * cap * VS
    PB = VS * Y
    L4 = 4 * E
    travel = jnp.bfloat16 if (cap * VS) % 16 == 0 else jnp.float32
    vmem = pl.BlockSpec(memory_space=pltpu.VMEM)
    dma = pltpu.SemaphoreType.DMA
    flow, stored = pl.pallas_call(
        functools.partial(kernel, sizes),
        out_shape=(
            jax.ShapeDtypeStruct(velocity.shape, jnp.float32),
            jax.ShapeDtypeStruct((L4, NODES), jnp.float32),
        ),
        in_specs=[vmem] * 6,
        out_specs=(vmem, vmem),
        scratch_shapes=[
            pltpu.VMEM((2, 3, X + 2, Y, Z), jnp.float32),
            pltpu.VMEM((2, 2, 3, X, Z), jnp.float32),
            pltpu.VMEM((2, 2, 3, X, Z), jnp.float32),
            pltpu.VMEM((2, 2, Y, Z), jnp.float32),
            pltpu.VMEM((2, 2, Y, Z), jnp.float32),
            pltpu.VMEM((2, 6, FACE, L4), jnp.bfloat16),
            pltpu.VMEM((2, 6, FACE, L4), jnp.bfloat16),
            pltpu.VMEM((2, peers, cap * VS, 4 * PB), travel),
            pltpu.VMEM((2, peers, cap * VS, 4 * PB), travel),
            pltpu.VMEM((NODES, L4), jnp.float32),
            pltpu.VMEM((NODES, L4), jnp.float32),
            pltpu.VMEM((X // (2 * VS), 4 * PB, Z), jnp.float32),
            pltpu.VMEM((R, NV * 2 * VS), jnp.bfloat16),
            pltpu.VMEM((VS * E, R), jnp.bfloat16),
            pltpu.VMEM((NODES, 2 * VS * PB), jnp.bfloat16),
            dma((2, 6)), dma((2, 6)), dma((2, 6)), dma((2, 6)),
            dma((2, peers - 1)), dma((2, peers - 1)),
        ],
        compiler_params=pltpu.CompilerParams(
            collective_id=0, has_side_effects=True, vmem_limit_bytes=32 * 1024 * 1024
        ),
    )(
        velocity, acoustic.reshape(L4, NODES), projection, owner_index, slot_element, element_cell
    )
    return flow, stored.reshape(acoustic.shape)


def solution(mesh):
    in_specs = (
        P(None, "gx", "gy", "gz"),
        P(("gx", "gy", "gz"), None, None),
        P(),
        P(("gx", "gy", "gz"), None),
        P(("gx", "gy", "gz"), None),
        P(("gx", "gy", "gz"), None),
    )
    out_specs = (P(None, "gx", "gy", "gz"), P(("gx", "gy", "gz"), None, None))
    return jax.shard_map(
        on_device, mesh=mesh, in_specs=in_specs, out_specs=out_specs, check_vma=False
    )
```

```python
import functools

import jax
import jax.numpy as jnp
import numpy as np
from jax import lax
from jax.experimental import pallas as pl
from jax.experimental.pallas import tpu as pltpu
from jax.sharding import PartitionSpec as P

VS = 4
ORDER = 7
EBX = 1
EBY = 2
EBZ = 16
K = ORDER + 1
FACE = K * K
NODES = K**3

HIGHEST = lax.Precision.HIGHEST
FLOW_STEP = 0.1
VISCOSITY = 0.05
WAVE_STEP = 0.02
SOURCE_GAIN = 25.0
MESH = pl.DeviceIdType.MESH


def legendre_table(points, order):
    columns = [points * 0.0 + 1.0, points]
    for degree in range(2, order + 1):
        columns.append(
            ((2 * degree - 1) * points * columns[degree - 1] - (degree - 1) * columns[degree - 2])
            / degree
        )
    return np.stack(columns, axis=1)


def lobatto_tables(order):
    point_count = order + 1
    points = -np.cos(np.pi * np.arange(point_count) / order)
    for newton_step in range(60):
        legendre = legendre_table(points, order)
        points = points - (points * legendre[:, order] - legendre[:, order - 1]) / (
            point_count * legendre[:, order]
        )
    legendre = legendre_table(points, order)
    highest = legendre[:, order]
    spacing = points[:, None] - points[None, :] + np.eye(point_count)
    derivative = highest[:, None] / (highest[None, :] * spacing)
    derivative = derivative * (1.0 - np.eye(point_count))
    derivative[0, 0] = -order * point_count / 4.0
    derivative[order, order] = order * point_count / 4.0
    return derivative


def iota(shape, axis):
    return lax.broadcasted_iota(jnp.int32, shape, axis)


def as_float(mask):
    return jnp.where(mask, 1.0, 0.0).astype(jnp.float32)


def to_column(row, count):
    eye = iota((count, count), 0) == iota((count, count), 1)
    return jnp.sum(jnp.where(eye, row, 0.0), axis=1, keepdims=True)


def spread_row(column, count, width, group):
    pick = iota((count, width), 0) == iota((count, width), 1) // group
    return jnp.sum(jnp.where(pick, column, 0.0), axis=0, keepdims=True)


def split(value):
    high = value.astype(jnp.bfloat16)
    low = (value - high.astype(jnp.float32)).astype(jnp.bfloat16)
    return high, low


def dot(a, b, contract=((1,), (0,)), precision=None):
    return lax.dot_general(
        a, b, (contract, ((), ())), preferred_element_type=jnp.float32, precision=precision
    )


def permutation(cell_row, elements):
    total = 4 * elements
    rows = iota((total, elements), 0)
    cell = jnp.sum(
        jnp.where(iota((total, elements), 1) == rows % elements, cell_row, 0.0),
        axis=1, keepdims=True,
    )
    r = iota((total, total), 0)
    goal = (r - r % elements).astype(jnp.float32) + cell
    return as_float(iota((total, total), 1).astype(jnp.float32) == goal).astype(jnp.bfloat16)


def swap(value, group, along, width):
    axis = value.ndim - 1
    total = 4 * width
    here = (1 + along) * width
    up = pltpu.roll(value, here, axis)
    down = up if 2 * here == total else pltpu.roll(value, total - here, axis)
    return jnp.where(group == 0, down, jnp.where(group == 1 + along, up, 0.0))


def derive(values, table):
    half = K // 2
    even = [values[j] + values[K - 1 - j] for j in range(half)]
    odd = [values[j] - values[K - 1 - j] for j in range(half)]
    result = [None] * K
    for a in range(half):
        first = sum(
            float(0.5 * (table[a, j] - table[a, K - 1 - j])) * odd[j] for j in range(half)
        )
        second = sum(
            float(0.5 * (table[a, j] + table[a, K - 1 - j])) * even[j] for j in range(half)
        )
        result[a] = first + second
        result[K - 1 - a] = first - second
    return result


def kernel(
    sizes,
    u_in, ac_in, proj_in, owner_in, slot_in, cell_in,
    u_out, ac_out,
    flow, y_send, y_recv, z_send, z_recv, tr_send, tr_recv, vol_send, vol_recv,
    q_ref, acc, lhs, place, gather, proj_ref,
    v_ssem, v_rsem, t_ssem, t_rsem, p_ssem, p_rsem,
):
    nx, ny, nz, X, Y, Z, E, NV, cap = sizes
    peers = ny * nz
    gx, gy, gz = lax.axis_index("gx"), lax.axis_index("gy"), lax.axis_index("gz")
    me = gy * nz + gz
    across = [
        {"gx": lax.rem(gx + nx - 1, nx)}, {"gx": lax.rem(gx + 1, nx)},
        {"gy": lax.rem(gy + ny - 1, ny)}, {"gy": lax.rem(gy + 1, ny)},
        {"gz": lax.rem(gz + nz - 1, nz)}, {"gz": lax.rem(gz + 1, nz)},
    ]
    others = []
    for k in range(1, peers):
        p = lax.rem(me + k, peers)
        others.append((p, {"gy": lax.div(p, nz), "gz": lax.rem(p, nz)}))

    barrier = pltpu.get_barrier_semaphore()
    for target in across[:2] + [t for _, t in others]:
        pl.semaphore_signal(barrier, inc=1, device_id=target, device_id_type=MESH)

    lane = iota((Y, Z), 1)
    sub = iota((Y, Z), 0)

    def pack(t, x, values, carry):
        low, high = carry
        for c in range(3):
            at = c * X + x
            low = jnp.where(lane == at, pltpu.roll(values[c], at, 1), low)
            high = jnp.where(lane == at, pltpu.roll(values[c], at + 1, 1), high)
            y_send[t, 0, c, pl.ds(x, 1), :] = values[c][0:1]
            y_send[t, 1, c, pl.ds(x, 1), :] = values[c][Y - 1:Y]
        return low, high

    def fill(x, carry):
        values = [u_in[c, x] for c in range(3)]
        for c in range(3):
            flow[0, c, x + 1] = values[c]
        return pack(0, x, values, carry)

    blank = jnp.zeros((Y, Z), jnp.float32)

    def velocity_copies(t):
        result = []
        for f in range(6):
            s = f % 2
            if f < 2:
                src = flow.at[t, :, X if s else 1]
                dst = flow.at[t, :, 0 if s else X + 1]
            elif f < 4:
                src, dst = y_send.at[t, s], y_recv.at[t, 1 - s]
            else:
                src, dst = z_send.at[t, s], z_recv.at[t, 1 - s]
            result.append(
                pltpu.make_async_remote_copy(
                    src_ref=src, dst_ref=dst, send_sem=v_ssem.at[t, f],
                    recv_sem=v_rsem.at[t, f ^ 1], device_id=across[f], device_id_type=MESH,
                )
            )
        return result

    def trace_copies(t):
        return [
            pltpu.make_async_remote_copy(
                src_ref=tr_send.at[t, f], dst_ref=tr_recv.at[t, f ^ 1],
                send_sem=t_ssem.at[t, f], recv_sem=t_rsem.at[t, f ^ 1],
                device_id=across[f], device_id_type=MESH,
            )
            for f in range(6)
        ]

    def volume_copies(t):
        return [
            pltpu.make_async_remote_copy(
                src_ref=vol_send.at[t, p], dst_ref=vol_recv.at[t, me],
                send_sem=p_ssem.at[t, k], recv_sem=p_rsem.at[t, k],
                device_id=target, device_id_type=MESH,
            )
            for k, (p, target) in enumerate(others)
        ]

    low, high = lax.fori_loop(0, X, fill, (blank, blank), unroll=True)
    z_send[0, 0] = low
    z_send[0, 1] = high
    pl.semaphore_wait(barrier, peers + 1)
    v0 = velocity_copies(0)
    for f in (0, 1, 4, 5, 2, 3):
        v0[f].start()

    L4 = 4 * E
    cell_row = cell_in[...].astype(jnp.float32)
    perm = permutation(cell_row, E)
    blocks = NODES // L4
    stored = []
    for j in range(blocks):
        parts = [ac_in[pl.ds(4 * j + v, E, stride=4 * blocks), :] for v in range(4)]
        stored.append(jnp.concatenate(parts, axis=0).T)
    ah, al = split(jnp.concatenate(stored, axis=0))
    q_ref[...] = dot(
        jnp.concatenate([ah, al], axis=1), jnp.concatenate([perm, perm], axis=0)
    )

    def trace(f):
        a, s = f // 2, f % 2
        if a == 0:
            return q_ref[s * (K - 1) * FACE:s * (K - 1) * FACE + FACE, :]
        if a == 1:
            base = s * (K - 1) * K
            return jnp.concatenate(
                [q_ref[i * FACE + base:i * FACE + base + K, :] for i in range(K)], axis=0
            )
        return q_ref[pl.ds(s * (K - 1), FACE, stride=K), :]

    def send_traces(t):
        for f in range(6):
            tr_send[t, f] = trace(f).astype(jnp.bfloat16)
        copies = trace_copies(t)
        for copy in copies:
            copy.start()
        return copies

    t0 = send_traces(0)

    cells = VS**3
    own_row = owner_in[...].astype(jnp.float32)
    own = to_column(own_row, NV)
    matches = (own == own_row) & (iota((NV, NV), 1) < iota((NV, NV), 0))
    rank = jnp.sum(as_float(matches), axis=1, keepdims=True)
    slot_of = own * float(cap) + rank
    W = NV * 2 * VS
    R = peers * cap * VS
    slot_row = spread_row(slot_of, NV, W, 2 * VS)
    wl = iota((1, W), 1)
    goal = slot_row * float(VS) + ((wl % (2 * VS)) // 2).astype(jnp.float32)
    goal = jnp.where(wl % 2 == 0, goal, -1.0)
    place[...] = as_float(iota((R, W), 0).astype(jnp.float32) == goal).astype(jnp.bfloat16)

    slots = peers * cap
    slot_col = to_column(slot_in[...].astype(jnp.float32), slots)
    element_row = spread_row(slot_col, slots, R, VS)
    cell_col = to_column(cell_row, E)
    target_row = jnp.sum(
        jnp.where(iota((E, R), 0).astype(jnp.float32) == element_row, cell_col, 0.0),
        axis=0, keepdims=True,
    )
    goal = target_row + ((iota((1, R), 1) % VS) * E).astype(jnp.float32)
    gather[...] = as_float(iota((VS * E, R), 0).astype(jnp.float32) == goal).astype(jnp.bfloat16)

    PB = VS * Y
    pr = iota((VS * PB, cells), 0)
    pc = iota((VS * PB, cells), 1)
    source_cell = ((pr % PB) // Y * VS + (pr % Y) // 2) * VS + pr // PB
    select = as_float((source_cell == pc) & (pr % 2 == 0)) * (-WAVE_STEP * SOURCE_GAIN)
    arranged = dot(select, proj_in[...], precision=HIGHEST).T
    ph, plo = split(arranged)
    proj_ref[:, :VS * PB] = ph
    proj_ref[:, VS * PB:] = plo

    table = -WAVE_STEP * lobatto_tables(ORDER)
    group3 = iota((K, K, L4), 2) // E
    group2 = iota((FACE, L4), 1) // E
    sub3 = iota((K, K, L4), 1)

    def local_rates():
        factors = []
        subl = iota((K, L4), 0)
        for k in range(K):
            factor = jnp.zeros((K, L4), jnp.float32)
            for c in range(K):
                factor = jnp.where(subl == c, float(table[c, (c - k) % K]), factor)
            factors.append(factor)

        def first(i, carry):
            at = pl.multiple_of(i * FACE, FACE)
            x = q_ref[pl.ds(at, FACE), :].reshape(K, K, L4)
            total = x
            s2 = swap(x, group3, 2, E)
            for k in range(K):
                rolled = s2 if k == 0 else pltpu.roll(s2, k, 1)
                total = total + factors[k][None] * rolled
            s1 = swap(x, group3, 1, E)
            parts = derive([s1[j] for j in range(K)], table)
            total = total + jnp.stack(parts)
            acc[pl.ds(at, FACE), :] = total.reshape(FACE, L4)
            return carry

        lax.fori_loop(0, K, first, 0, unroll=True)

        def second(i, carry):
            ats = [pl.multiple_of(a * FACE + i * K, K) for a in range(K)]
            x = jnp.stack([q_ref[pl.ds(at, K), :] for at in ats])
            s0 = swap(x, group3, 0, E)
            parts = derive([s0[j] for j in range(K)], table)
            for at, part in zip(ats, parts):
                acc[pl.ds(at, K), :] += part
            return carry

        lax.fori_loop(0, K, second, 0, unroll=True)

    lane2 = iota((FACE, L4), 1)
    y_of = (lane2 % E) // EBZ
    z_of = lane2 % EBZ
    scale = WAVE_STEP * 0.5 * ORDER * (ORDER + 1) / 2.0

    def add_flux(t):
        for f in range(6):
            a, s = f // 2, f % 2
            inner = trace(f)
            other = tr_recv[t, f].astype(jnp.float32)
            if a == 0:
                outer = other
            elif a == 1:
                mine = trace(f ^ 1)
                edge = 0 if s else EBY - 1
                mixed = jnp.where(y_of == edge, other, mine)
                near = EBZ if s == 0 else L4 - EBZ
                wrap = (L4 - (EBY - 1) * EBZ) if s == 0 else (EBY - 1) * EBZ
                outer = jnp.where(
                    y_of == (EBY - 1 if s else 0),
                    pltpu.roll(mixed, wrap, 1), pltpu.roll(mixed, near, 1),
                )
            else:
                mine = trace(f ^ 1)
                edge = 0 if s else EBZ - 1
                mixed = jnp.where(z_of == edge, other, mine)
                near = 1 if s == 0 else L4 - 1
                wrap = (L4 - (EBZ - 1)) if s == 0 else EBZ - 1
                outer = jnp.where(
                    z_of == (EBZ - 1 if s else 0),
                    pltpu.roll(mixed, wrap, 1), pltpu.roll(mixed, near, 1),
                )
            jump = inner - outer
            turned = swap(jump, group2, a, E)
            flux = scale * ((turned if s else -turned) - jump)
            if a == 0:
                base = s * (K - 1) * FACE
                acc[base:base + FACE, :] += flux
            elif a == 1:
                base = s * (K - 1) * K
                for i in range(K):
                    at = i * FACE + base
                    acc[at:at + K, :] += flux[i * K:(i + 1) * K]
            else:
                where = pl.ds(s * (K - 1), FACE, stride=K)
                acc[where, :] = acc[where, :] + flux

    def flow_step(t):
        z_low = z_recv[t, 0]
        z_high = z_recv[t, 1]

        def column(x, carry):
            centre = [flow[t, c, x + 1] for c in range(3)]
            below, above = [], []
            for c in range(3):
                at = c * X + x
                u = centre[c]
                pair = (flow[t, c, x], flow[t, c, x + 2])
                y_low = y_recv[t, 0, c, pl.ds(x, 1), :]
                y_high = y_recv[t, 1, c, pl.ds(x, 1), :]
                ym = jnp.where(sub == 0, y_low, pltpu.roll(u, 1, 0))
                yp = jnp.where(sub == Y - 1, y_high, pltpu.roll(u, Y - 1, 0))
                zm = jnp.where(
                    lane == 0, pltpu.roll(z_low, lax.rem(Z - at, Z), 1), pltpu.roll(u, 1, 1)
                )
                zp = jnp.where(
                    lane == Z - 1, pltpu.roll(z_high, Z - 1 - at, 1), pltpu.roll(u, Z - 1, 1)
                )
                below.append((pair[0], ym, zm))
                above.append((pair[1], yp, zp))
            slope = [[0.5 * (above[c][a] - below[c][a]) for c in range(3)] for a in range(3)]
            updated = []
            for c in range(3):
                rate = VISCOSITY * (
                    (above[c][0] + below[c][0])
                    + (above[c][1] + below[c][1])
                    + (above[c][2] + below[c][2])
                    - 6.0 * centre[c]
                )
                for a in range(3):
                    rate = rate - centre[a] * slope[a][c]
                updated.append(centre[c] + FLOW_STEP * rate)
            w = [
                slope[1][2] - slope[2][1], slope[2][0] - slope[0][2], slope[0][1] - slope[1][0]
            ]
            lamb = [
                w[1] * centre[2] - w[2] * centre[1],
                w[2] * centre[0] - w[0] * centre[2],
                w[0] * centre[1] - w[1] * centre[0],
            ]
            if t == 0:
                for c in range(3):
                    flow[1, c, x + 1] = updated[c]
                carry = pack(1, x, updated, carry)
            else:
                for c in range(3):
                    u_out[c, x] = updated[c]
            return lamb, carry

        def couple(i, carry):
            first, carry = column(2 * i, carry)
            second, carry = column(2 * i + 1, carry)
            block = lax.div(i, VS)
            row = lax.rem(i, VS)
            for c in range(3):
                total = first[c] + second[c]
                total = total + pltpu.roll(total, Y - 1, 0)
                total = total + pltpu.roll(total, Z - 1, 1)
                at = pl.multiple_of(c * PB + row * Y, Y)
                lhs[block, pl.ds(at, Y), :] = 0.125 * total
            return carry

        carry = lax.fori_loop(0, X // 2, couple, (blank, blank), unroll=True)
        if t == 0:
            z_send[1, 0] = carry[0]
            z_send[1, 1] = carry[1]

    def send_volumes(t):
        wide = jnp.concatenate([lhs[i] for i in range(X // (2 * VS))], axis=1)
        sent = dot(place[...], wide.astype(jnp.bfloat16), ((1,), (1,)))
        vol_send[t] = sent.astype(vol_send.dtype).reshape(peers, cap * VS, 4 * PB)
        copies = volume_copies(t)
        for copy in copies:
            copy.start()
        vol_recv[t, me] = vol_send[t, me]
        return copies

    def add_source(t):
        received = vol_recv[t].reshape(R, 4 * PB).astype(jnp.bfloat16)
        summed = dot(gather[...], received).T
        group = iota((PB, L4), 1) // E
        blocks = []
        for c in range(VS):
            block = jnp.zeros((PB, L4), jnp.float32)
            for v in range(3):
                part = summed[v * PB:(v + 1) * PB]
                shift = ((1 + v - c) * E) % L4
                if shift:
                    part = pltpu.roll(part, shift, 1)
                block = jnp.where(group == 1 + v, part, block)
            blocks.append(block)
        bh, bl = split(jnp.concatenate(blocks, axis=0))
        source = dot(proj_ref[...], jnp.concatenate([bh, bh], axis=0))
        source = source + dot(proj_ref[:, :VS * PB], bl)
        acc[...] = acc[...] + source

    lhs[...] = jnp.zeros_like(lhs)
    for copy in v0:
        copy.wait_recv()
    flow_step(0)
    p0 = send_volumes(0)
    v1 = velocity_copies(1)
    for f in (0, 1, 4, 5, 2, 3):
        v1[f].start()
    local_rates()
    for copy in t0:
        copy.wait_recv()
    add_flux(0)
    for copy in v1:
        copy.wait_recv()
    flow_step(1)
    p1 = send_volumes(1)
    for copy in p0:
        copy.wait_recv()
    add_source(0)
    q_ref[...] = acc[...]
    t1 = send_traces(1)
    local_rates()
    for copy in p1:
        copy.wait_recv()
    add_source(1)
    for copy in t1:
        copy.wait_recv()
    add_flux(1)
    ac_out[...] = acc[...]
    for copies in (v0, t0, p0, v1, t1, p1):
        for copy in copies:
            copy.wait_send()


def finish(u_in, q_in, cell_in, u_hbm, ac_hbm, ac_out, sems):
    flow_copy = pltpu.make_async_copy(u_in, u_hbm, sems.at[0])
    flow_copy.start()
    nodes, total = q_in.shape
    E = total // 4
    perm = permutation(cell_in[...].astype(jnp.float32), E)
    high, low = split(q_in[...])
    stored = dot(
        jnp.concatenate([perm, perm], axis=1), jnp.concatenate([high, low], axis=1), ((1,), (1,))
    )
    blocks = nodes // total
    for j in range(blocks):
        for v in range(4):
            ac_out[pl.ds(4 * j + v, E, stride=4 * blocks), :] = stored[
                v * E:(v + 1) * E, j * total:(j + 1) * total
            ]
    wave_copy = pltpu.make_async_copy(ac_out, ac_hbm, sems.at[1])
    wave_copy.start()
    flow_copy.wait()
    wave_copy.wait()


def on_device(velocity, acoustic, projection, owner_index, slot_element, element_cell):
    nx, ny, nz = lax.axis_size("gx"), lax.axis_size("gy"), lax.axis_size("gz")
    _, X, Y, Z = velocity.shape
    E = acoustic.shape[0]
    NV = owner_index.shape[0]
    peers = ny * nz
    cap = slot_element.shape[1] // peers
    sizes = (nx, ny, nz, X, Y, Z, E, NV, cap)
    R = peers * cap * VS
    PB = VS * Y
    L4 = 4 * E
    travel = jnp.bfloat16 if (cap * VS) % 16 == 0 else jnp.float32
    vmem = pl.BlockSpec(memory_space=pltpu.VMEM)
    hbm = pl.BlockSpec(memory_space=pltpu.HBM)
    dma = pltpu.SemaphoreType.DMA
    blocks = NODES // L4
    cells = acoustic.reshape(E, 4, blocks, L4).transpose(0, 2, 1, 3).reshape(NODES, L4)
    flow, wave = pl.pallas_call(
        functools.partial(kernel, sizes),
        out_shape=(
            jax.ShapeDtypeStruct(velocity.shape, jnp.float32),
            jax.ShapeDtypeStruct((NODES, L4), jnp.float32),
        ),
        in_specs=[vmem] * 6,
        out_specs=(vmem, vmem),
        scratch_shapes=[
            pltpu.VMEM((2, 3, X + 2, Y, Z), jnp.float32),
            pltpu.VMEM((2, 2, 3, X, Z), jnp.float32),
            pltpu.VMEM((2, 2, 3, X, Z), jnp.float32),
            pltpu.VMEM((2, 2, Y, Z), jnp.float32),
            pltpu.VMEM((2, 2, Y, Z), jnp.float32),
            pltpu.VMEM((2, 6, FACE, L4), jnp.bfloat16),
            pltpu.VMEM((2, 6, FACE, L4), jnp.bfloat16),
            pltpu.VMEM((2, peers, cap * VS, 4 * PB), travel),
            pltpu.VMEM((2, peers, cap * VS, 4 * PB), travel),
            pltpu.VMEM((NODES, L4), jnp.float32),
            pltpu.VMEM((NODES, L4), jnp.float32),
            pltpu.VMEM((X // (2 * VS), 4 * PB, Z), jnp.float32),
            pltpu.VMEM((R, NV * 2 * VS), jnp.bfloat16),
            pltpu.VMEM((VS * E, R), jnp.bfloat16),
            pltpu.VMEM((NODES, 2 * VS * PB), jnp.bfloat16),
            dma((2, 6)), dma((2, 6)), dma((2, 6)), dma((2, 6)),
            dma((2, peers - 1)), dma((2, peers - 1)),
        ],
        compiler_params=pltpu.CompilerParams(
            collective_id=0, has_side_effects=True, vmem_limit_bytes=32 * 1024 * 1024
        ),
    )(
        velocity, cells, projection, owner_index.reshape(1, NV), slot_element, element_cell
    )
    flow, stored = pl.pallas_call(
        finish,
        out_shape=(
            jax.ShapeDtypeStruct(velocity.shape, jnp.float32),
            jax.ShapeDtypeStruct((NODES, L4), jnp.float32),
        ),
        in_specs=[vmem] * 3,
        out_specs=(hbm, hbm),
        scratch_shapes=[pltpu.VMEM((NODES, L4), jnp.float32), dma((2,))],
    )(flow, wave, element_cell)
    stored = stored.reshape(E, blocks, 4, L4).transpose(0, 2, 1, 3).reshape(acoustic.shape)
    return flow, stored


def solution(mesh):
    in_specs = (
        P(None, "gx", "gy", "gz"),
        P(("gx", "gy", "gz"), None, None),
        P(),
        P(("gx", "gy", "gz"), None),
        P(("gx", "gy", "gz"), None),
        P(("gx", "gy", "gz"), None),
    )
    out_specs = (P(None, "gx", "gy", "gz"), P(("gx", "gy", "gz"), None, None))
    return jax.shard_map(
        on_device, mesh=mesh, in_specs=in_specs, out_specs=out_specs, check_vma=False
    )
```

```python
import functools

import jax
import jax.numpy as jnp
import numpy as np
from jax import lax
from jax.experimental import pallas as pl
from jax.experimental.pallas import tpu as pltpu
from jax.sharding import PartitionSpec as P

VS = 4
ORDER = 7
EBX = 1
EBY = 2
EBZ = 16
K = ORDER + 1
FACE = K * K
NODES = K**3

HIGHEST = lax.Precision.HIGHEST
FLOW_STEP = 0.1
VISCOSITY = 0.05
WAVE_STEP = 0.02
SOURCE_GAIN = 25.0
MESH = pl.DeviceIdType.MESH


def legendre_table(points, order):
    columns = [points * 0.0 + 1.0, points]
    for degree in range(2, order + 1):
        columns.append(
            ((2 * degree - 1) * points * columns[degree - 1] - (degree - 1) * columns[degree - 2])
            / degree
        )
    return np.stack(columns, axis=1)


def lobatto_tables(order):
    point_count = order + 1
    points = -np.cos(np.pi * np.arange(point_count) / order)
    for newton_step in range(60):
        legendre = legendre_table(points, order)
        points = points - (points * legendre[:, order] - legendre[:, order - 1]) / (
            point_count * legendre[:, order]
        )
    legendre = legendre_table(points, order)
    highest = legendre[:, order]
    spacing = points[:, None] - points[None, :] + np.eye(point_count)
    derivative = highest[:, None] / (highest[None, :] * spacing)
    derivative = derivative * (1.0 - np.eye(point_count))
    derivative[0, 0] = -order * point_count / 4.0
    derivative[order, order] = order * point_count / 4.0
    return derivative


def iota(shape, axis):
    return lax.broadcasted_iota(jnp.int32, shape, axis)


def as_float(mask):
    return jnp.where(mask, 1.0, 0.0).astype(jnp.float32)


def to_column(row, count):
    eye = iota((count, count), 0) == iota((count, count), 1)
    return jnp.sum(jnp.where(eye, row, 0.0), axis=1, keepdims=True)


def spread_row(column, count, width, group):
    pick = iota((count, width), 0) == iota((count, width), 1) // group
    return jnp.sum(jnp.where(pick, column, 0.0), axis=0, keepdims=True)


def split(value):
    high = value.astype(jnp.bfloat16)
    low = (value - high.astype(jnp.float32)).astype(jnp.bfloat16)
    return high, low


def dot(a, b, contract=((1,), (0,)), precision=None):
    return lax.dot_general(
        a, b, (contract, ((), ())), preferred_element_type=jnp.float32, precision=precision
    )


def permutation(cell_row, elements):
    total = 4 * elements
    rows = iota((total, elements), 0)
    cell = jnp.sum(
        jnp.where(iota((total, elements), 1) == rows % elements, cell_row, 0.0),
        axis=1, keepdims=True,
    )
    r = iota((total, total), 0)
    goal = (r - r % elements).astype(jnp.float32) + cell
    return as_float(iota((total, total), 1).astype(jnp.float32) == goal).astype(jnp.bfloat16)


def swap(value, group, along, width):
    axis = value.ndim - 1
    total = 4 * width
    here = (1 + along) * width
    up = pltpu.roll(value, here, axis)
    down = up if 2 * here == total else pltpu.roll(value, total - here, axis)
    return jnp.where(group == 0, down, jnp.where(group == 1 + along, up, 0.0))


def derive(values, table):
    half = K // 2
    even = [values[j] + values[K - 1 - j] for j in range(half)]
    odd = [values[j] - values[K - 1 - j] for j in range(half)]
    result = [None] * K
    for a in range(half):
        first = sum(
            float(0.5 * (table[a, j] - table[a, K - 1 - j])) * odd[j] for j in range(half)
        )
        second = sum(
            float(0.5 * (table[a, j] + table[a, K - 1 - j])) * even[j] for j in range(half)
        )
        result[a] = first + second
        result[K - 1 - a] = first - second
    return result


def kernel(
    sizes,
    u_hbm, ac_hbm, proj_hbm, owner_hbm, slot_hbm, cell_hbm,
    u_out, ac_out, perm_out,
    u_in, ac_in, proj_in, owner_in, slot_in, cell_in, in_sems, flow, y_send, y_recv, z_send, z_recv, tr_send, tr_recv, vol_send, vol_recv,
    q_ref, acc, lhs, place, gather, proj_ref,
    v_ssem, v_rsem, t_ssem, t_rsem, p_ssem, p_rsem,
):
    nx, ny, nz, X, Y, Z, E, NV, cap = sizes
    peers = ny * nz
    gx, gy, gz = lax.axis_index("gx"), lax.axis_index("gy"), lax.axis_index("gz")
    me = gy * nz + gz
    across = [
        {"gx": lax.rem(gx + nx - 1, nx)}, {"gx": lax.rem(gx + 1, nx)},
        {"gy": lax.rem(gy + ny - 1, ny)}, {"gy": lax.rem(gy + 1, ny)},
        {"gz": lax.rem(gz + nz - 1, nz)}, {"gz": lax.rem(gz + 1, nz)},
    ]
    others = []
    for k in range(1, peers):
        p = lax.rem(me + k, peers)
        others.append((p, {"gy": lax.div(p, nz), "gz": lax.rem(p, nz)}))

    barrier = pltpu.get_barrier_semaphore()
    for target in across[:2] + [t for _, t in others]:
        pl.semaphore_signal(barrier, inc=1, device_id=target, device_id_type=MESH)

    sources = (u_hbm, cell_hbm, ac_hbm, owner_hbm, slot_hbm, proj_hbm)
    targets = (u_in, cell_in, ac_in, owner_in, slot_in, proj_in)
    loads = [
        pltpu.make_async_copy(src, dst, in_sems.at[i])
        for i, (src, dst) in enumerate(zip(sources, targets))
    ]
    for load in loads:
        load.start()

    lane = iota((Y, Z), 1)
    sub = iota((Y, Z), 0)

    def pack(t, x, values, carry):
        low, high = carry
        for c in range(3):
            at = c * X + x
            low = jnp.where(lane == at, pltpu.roll(values[c], at, 1), low)
            high = jnp.where(lane == at, pltpu.roll(values[c], at + 1, 1), high)
            y_send[t, 0, c, pl.ds(x, 1), :] = values[c][0:1]
            y_send[t, 1, c, pl.ds(x, 1), :] = values[c][Y - 1:Y]
        return low, high

    def fill(x, carry):
        values = [u_in[c, x] for c in range(3)]
        for c in range(3):
            flow[0, c, x + 1] = values[c]
        return pack(0, x, values, carry)

    blank = jnp.zeros((Y, Z), jnp.float32)

    def velocity_copies(t):
        result = []
        for f in range(6):
            s = f % 2
            if f < 2:
                src = flow.at[t, :, X if s else 1]
                dst = flow.at[t, :, 0 if s else X + 1]
            elif f < 4:
                src, dst = y_send.at[t, s], y_recv.at[t, 1 - s]
            else:
                src, dst = z_send.at[t, s], z_recv.at[t, 1 - s]
            result.append(
                pltpu.make_async_remote_copy(
                    src_ref=src, dst_ref=dst, send_sem=v_ssem.at[t, f],
                    recv_sem=v_rsem.at[t, f ^ 1], device_id=across[f], device_id_type=MESH,
                )
            )
        return result

    def trace_copies(t):
        return [
            pltpu.make_async_remote_copy(
                src_ref=tr_send.at[t, f], dst_ref=tr_recv.at[t, f ^ 1],
                send_sem=t_ssem.at[t, f], recv_sem=t_rsem.at[t, f ^ 1],
                device_id=across[f], device_id_type=MESH,
            )
            for f in range(6)
        ]

    def volume_copies(t):
        return [
            pltpu.make_async_remote_copy(
                src_ref=vol_send.at[t, p], dst_ref=vol_recv.at[t, me],
                send_sem=p_ssem.at[t, k], recv_sem=p_rsem.at[t, k],
                device_id=target, device_id_type=MESH,
            )
            for k, (p, target) in enumerate(others)
        ]

    loads[0].wait()
    low, high = lax.fori_loop(0, X, fill, (blank, blank), unroll=True)
    z_send[0, 0] = low
    z_send[0, 1] = high
    pl.semaphore_wait(barrier, peers + 1)
    v0 = velocity_copies(0)
    for f in (0, 1, 4, 5, 2, 3):
        v0[f].start()

    L4 = 4 * E
    loads[1].wait()
    loads[2].wait()
    cell_row = cell_in[...].astype(jnp.float32)
    perm = permutation(cell_row, E)
    perm_out[...] = perm
    blocks = NODES // L4
    stored = []
    for j in range(blocks):
        parts = [ac_in[pl.ds(4 * j + v, E, stride=4 * blocks), :] for v in range(4)]
        stored.append(jnp.concatenate(parts, axis=0).T)
    ah, al = split(jnp.concatenate(stored, axis=0))
    q_ref[...] = dot(
        jnp.concatenate([ah, al], axis=1), jnp.concatenate([perm, perm], axis=0)
    )

    def trace(f):
        a, s = f // 2, f % 2
        if a == 0:
            return q_ref[s * (K - 1) * FACE:s * (K - 1) * FACE + FACE, :]
        if a == 1:
            base = s * (K - 1) * K
            return jnp.concatenate(
                [q_ref[i * FACE + base:i * FACE + base + K, :] for i in range(K)], axis=0
            )
        return q_ref[pl.ds(s * (K - 1), FACE, stride=K), :]

    def send_traces(t):
        for f in range(6):
            tr_send[t, f] = trace(f).astype(jnp.bfloat16)
        copies = trace_copies(t)
        for copy in copies:
            copy.start()
        return copies

    t0 = send_traces(0)

    cells = VS**3
    for load in loads[3:]:
        load.wait()
    own_row = owner_in[...].astype(jnp.float32)
    own = to_column(own_row, NV)
    matches = (own == own_row) & (iota((NV, NV), 1) < iota((NV, NV), 0))
    rank = jnp.sum(as_float(matches), axis=1, keepdims=True)
    slot_of = own * float(cap) + rank
    W = NV * 2 * VS
    R = peers * cap * VS
    slot_row = spread_row(slot_of, NV, W, 2 * VS)
    wl = iota((1, W), 1)
    goal = slot_row * float(VS) + ((wl % (2 * VS)) // 2).astype(jnp.float32)
    goal = jnp.where(wl % 2 == 0, goal, -1.0)
    place[...] = as_float(iota((R, W), 0).astype(jnp.float32) == goal).astype(jnp.bfloat16)

    slots = peers * cap
    slot_col = to_column(slot_in[...].astype(jnp.float32), slots)
    element_row = spread_row(slot_col, slots, R, VS)
    cell_col = to_column(cell_row, E)
    target_row = jnp.sum(
        jnp.where(iota((E, R), 0).astype(jnp.float32) == element_row, cell_col, 0.0),
        axis=0, keepdims=True,
    )
    goal = target_row + ((iota((1, R), 1) % VS) * E).astype(jnp.float32)
    gather[...] = as_float(iota((VS * E, R), 0).astype(jnp.float32) == goal).astype(jnp.bfloat16)

    PB = VS * Y
    pr = iota((VS * PB, cells), 0)
    pc = iota((VS * PB, cells), 1)
    source_cell = ((pr % PB) // Y * VS + (pr % Y) // 2) * VS + pr // PB
    select = as_float((source_cell == pc) & (pr % 2 == 0)) * (-WAVE_STEP * SOURCE_GAIN)
    arranged = dot(select, proj_in[...], precision=HIGHEST).T
    ph, plo = split(arranged)
    proj_ref[:, :VS * PB] = ph
    proj_ref[:, VS * PB:] = plo

    table = -WAVE_STEP * lobatto_tables(ORDER)
    group3 = iota((K, K, L4), 2) // E
    group2 = iota((FACE, L4), 1) // E
    sub3 = iota((K, K, L4), 1)

    def local_rates():
        factors = []
        subl = iota((K, L4), 0)
        for k in range(K):
            factor = jnp.zeros((K, L4), jnp.float32)
            for c in range(K):
                factor = jnp.where(subl == c, float(table[c, (c - k) % K]), factor)
            factors.append(factor)

        def first(i, carry):
            at = pl.multiple_of(i * FACE, FACE)
            x = q_ref[pl.ds(at, FACE), :].reshape(K, K, L4)
            total = x
            s2 = swap(x, group3, 2, E)
            for k in range(K):
                rolled = s2 if k == 0 else pltpu.roll(s2, k, 1)
                total = total + factors[k][None] * rolled
            s1 = swap(x, group3, 1, E)
            parts = derive([s1[j] for j in range(K)], table)
            total = total + jnp.stack(parts)
            acc[pl.ds(at, FACE), :] = total.reshape(FACE, L4)
            return carry

        lax.fori_loop(0, K, first, 0, unroll=True)

        def second(i, carry):
            ats = [pl.multiple_of(a * FACE + i * K, K) for a in range(K)]
            x = jnp.stack([q_ref[pl.ds(at, K), :] for at in ats])
            s0 = swap(x, group3, 0, E)
            parts = derive([s0[j] for j in range(K)], table)
            for at, part in zip(ats, parts):
                acc[pl.ds(at, K), :] += part
            return carry

        lax.fori_loop(0, K, second, 0, unroll=True)

    lane2 = iota((FACE, L4), 1)
    y_of = (lane2 % E) // EBZ
    z_of = lane2 % EBZ
    scale = WAVE_STEP * 0.5 * ORDER * (ORDER + 1) / 2.0

    def add_flux(t):
        for f in range(6):
            a, s = f // 2, f % 2
            inner = trace(f)
            other = tr_recv[t, f].astype(jnp.float32)
            if a == 0:
                outer = other
            elif a == 1:
                mine = trace(f ^ 1)
                edge = 0 if s else EBY - 1
                mixed = jnp.where(y_of == edge, other, mine)
                near = EBZ if s == 0 else L4 - EBZ
                wrap = (L4 - (EBY - 1) * EBZ) if s == 0 else (EBY - 1) * EBZ
                outer = jnp.where(
                    y_of == (EBY - 1 if s else 0),
                    pltpu.roll(mixed, wrap, 1), pltpu.roll(mixed, near, 1),
                )
            else:
                mine = trace(f ^ 1)
                edge = 0 if s else EBZ - 1
                mixed = jnp.where(z_of == edge, other, mine)
                near = 1 if s == 0 else L4 - 1
                wrap = (L4 - (EBZ - 1)) if s == 0 else EBZ - 1
                outer = jnp.where(
                    z_of == (EBZ - 1 if s else 0),
                    pltpu.roll(mixed, wrap, 1), pltpu.roll(mixed, near, 1),
                )
            jump = inner - outer
            turned = swap(jump, group2, a, E)
            flux = scale * ((turned if s else -turned) - jump)
            if a == 0:
                base = s * (K - 1) * FACE
                acc[base:base + FACE, :] += flux
            elif a == 1:
                base = s * (K - 1) * K
                for i in range(K):
                    at = i * FACE + base
                    acc[at:at + K, :] += flux[i * K:(i + 1) * K]
            else:
                where = pl.ds(s * (K - 1), FACE, stride=K)
                acc[where, :] = acc[where, :] + flux

    def flow_step(t):
        z_low = z_recv[t, 0]
        z_high = z_recv[t, 1]

        def column(x, carry):
            centre = [flow[t, c, x + 1] for c in range(3)]
            below, above = [], []
            for c in range(3):
                at = c * X + x
                u = centre[c]
                pair = (flow[t, c, x], flow[t, c, x + 2])
                y_low = y_recv[t, 0, c, pl.ds(x, 1), :]
                y_high = y_recv[t, 1, c, pl.ds(x, 1), :]
                ym = jnp.where(sub == 0, y_low, pltpu.roll(u, 1, 0))
                yp = jnp.where(sub == Y - 1, y_high, pltpu.roll(u, Y - 1, 0))
                zm = jnp.where(
                    lane == 0, pltpu.roll(z_low, lax.rem(Z - at, Z), 1), pltpu.roll(u, 1, 1)
                )
                zp = jnp.where(
                    lane == Z - 1, pltpu.roll(z_high, Z - 1 - at, 1), pltpu.roll(u, Z - 1, 1)
                )
                below.append((pair[0], ym, zm))
                above.append((pair[1], yp, zp))
            slope = [[0.5 * (above[c][a] - below[c][a]) for c in range(3)] for a in range(3)]
            updated = []
            for c in range(3):
                rate = VISCOSITY * (
                    (above[c][0] + below[c][0])
                    + (above[c][1] + below[c][1])
                    + (above[c][2] + below[c][2])
                    - 6.0 * centre[c]
                )
                for a in range(3):
                    rate = rate - centre[a] * slope[a][c]
                updated.append(centre[c] + FLOW_STEP * rate)
            w = [
                slope[1][2] - slope[2][1], slope[2][0] - slope[0][2], slope[0][1] - slope[1][0]
            ]
            lamb = [
                w[1] * centre[2] - w[2] * centre[1],
                w[2] * centre[0] - w[0] * centre[2],
                w[0] * centre[1] - w[1] * centre[0],
            ]
            if t == 0:
                for c in range(3):
                    flow[1, c, x + 1] = updated[c]
                carry = pack(1, x, updated, carry)
            else:
                for c in range(3):
                    u_out[c, x] = updated[c]
            return lamb, carry

        def couple(i, carry):
            first, carry = column(2 * i, carry)
            second, carry = column(2 * i + 1, carry)
            block = lax.div(i, VS)
            row = lax.rem(i, VS)
            for c in range(3):
                total = first[c] + second[c]
                total = total + pltpu.roll(total, Y - 1, 0)
                total = total + pltpu.roll(total, Z - 1, 1)
                at = pl.multiple_of(c * PB + row * Y, Y)
                lhs[block, pl.ds(at, Y), :] = 0.125 * total
            return carry

        carry = lax.fori_loop(0, X // 2, couple, (blank, blank), unroll=True)
        if t == 0:
            z_send[1, 0] = carry[0]
            z_send[1, 1] = carry[1]

    def send_volumes(t):
        wide = jnp.concatenate([lhs[i] for i in range(X // (2 * VS))], axis=1)
        sent = dot(place[...], wide.astype(jnp.bfloat16), ((1,), (1,)))
        vol_send[t] = sent.astype(vol_send.dtype).reshape(peers, cap * VS, 4 * PB)
        copies = volume_copies(t)
        for copy in copies:
            copy.start()
        vol_recv[t, me] = vol_send[t, me]
        return copies

    def add_source(t):
        received = vol_recv[t].reshape(R, 4 * PB).astype(jnp.bfloat16)
        summed = dot(gather[...], received).T
        group = iota((PB, L4), 1) // E
        blocks = []
        for c in range(VS):
            block = jnp.zeros((PB, L4), jnp.float32)
            for v in range(3):
                part = summed[v * PB:(v + 1) * PB]
                shift = ((1 + v - c) * E) % L4
                if shift:
                    part = pltpu.roll(part, shift, 1)
                block = jnp.where(group == 1 + v, part, block)
            blocks.append(block)
        bh, bl = split(jnp.concatenate(blocks, axis=0))
        source = dot(proj_ref[...], jnp.concatenate([bh, bh], axis=0))
        source = source + dot(proj_ref[:, :VS * PB], bl)
        acc[...] = acc[...] + source

    lhs[...] = jnp.zeros_like(lhs)
    for copy in v0:
        copy.wait_recv()
    flow_step(0)
    p0 = send_volumes(0)
    v1 = velocity_copies(1)
    for f in (0, 1, 4, 5, 2, 3):
        v1[f].start()
    local_rates()
    for copy in t0:
        copy.wait_recv()
    add_flux(0)
    for copy in v1:
        copy.wait_recv()
    flow_step(1)
    p1 = send_volumes(1)
    for copy in p0:
        copy.wait_recv()
    add_source(0)
    q_ref[...] = acc[...]
    t1 = send_traces(1)
    local_rates()
    for copy in p1:
        copy.wait_recv()
    add_source(1)
    for copy in t1:
        copy.wait_recv()
    add_flux(1)
    ac_out[...] = acc[...]
    for copies in (v0, t0, p0, v1, t1, p1):
        for copy in copies:
            copy.wait_send()


def finish(u_in, q_in, perm_in, u_hbm, ac_hbm, ac_out, sems):
    flow_copy = pltpu.make_async_copy(u_in, u_hbm, sems.at[0])
    flow_copy.start()
    nodes, total = q_in.shape
    E = total // 4
    perm = perm_in[...]
    high, low = split(q_in[...])
    stored = dot(
        jnp.concatenate([perm, perm], axis=1), jnp.concatenate([high, low], axis=1), ((1,), (1,))
    )
    blocks = nodes // total
    for j in range(blocks):
        for v in range(4):
            ac_out[pl.ds(4 * j + v, E, stride=4 * blocks), :] = stored[
                v * E:(v + 1) * E, j * total:(j + 1) * total
            ]
    wave_copy = pltpu.make_async_copy(ac_out, ac_hbm, sems.at[1])
    wave_copy.start()
    flow_copy.wait()
    wave_copy.wait()


def on_device(velocity, acoustic, projection, owner_index, slot_element, element_cell):
    nx, ny, nz = lax.axis_size("gx"), lax.axis_size("gy"), lax.axis_size("gz")
    _, X, Y, Z = velocity.shape
    E = acoustic.shape[0]
    NV = owner_index.shape[0]
    peers = ny * nz
    cap = slot_element.shape[1] // peers
    sizes = (nx, ny, nz, X, Y, Z, E, NV, cap)
    R = peers * cap * VS
    PB = VS * Y
    L4 = 4 * E
    travel = jnp.bfloat16 if (cap * VS) % 16 == 0 else jnp.float32
    vmem = pl.BlockSpec(memory_space=pltpu.VMEM)
    hbm = pl.BlockSpec(memory_space=pltpu.HBM)
    dma = pltpu.SemaphoreType.DMA
    blocks = NODES // L4
    cells = acoustic.reshape(E, 4, blocks, L4).transpose(0, 2, 1, 3).reshape(NODES, L4)
    flow, wave, perm = pl.pallas_call(
        functools.partial(kernel, sizes),
        out_shape=(
            jax.ShapeDtypeStruct(velocity.shape, jnp.float32),
            jax.ShapeDtypeStruct((NODES, L4), jnp.float32),
            jax.ShapeDtypeStruct((L4, L4), jnp.bfloat16),
        ),
        in_specs=[hbm] * 6,
        out_specs=(vmem, vmem, vmem),
        scratch_shapes=[
            pltpu.VMEM(velocity.shape, jnp.float32),
            pltpu.VMEM((NODES, L4), jnp.float32),
            pltpu.VMEM(projection.shape, jnp.float32),
            pltpu.VMEM((1, NV), jnp.int32),
            pltpu.VMEM(slot_element.shape, jnp.int32),
            pltpu.VMEM(element_cell.shape, jnp.int32),
            dma((6,)),
            pltpu.VMEM((2, 3, X + 2, Y, Z), jnp.float32),
            pltpu.VMEM((2, 2, 3, X, Z), jnp.float32),
            pltpu.VMEM((2, 2, 3, X, Z), jnp.float32),
            pltpu.VMEM((2, 2, Y, Z), jnp.float32),
            pltpu.VMEM((2, 2, Y, Z), jnp.float32),
            pltpu.VMEM((2, 6, FACE, L4), jnp.bfloat16),
            pltpu.VMEM((2, 6, FACE, L4), jnp.bfloat16),
            pltpu.VMEM((2, peers, cap * VS, 4 * PB), travel),
            pltpu.VMEM((2, peers, cap * VS, 4 * PB), travel),
            pltpu.VMEM((NODES, L4), jnp.float32),
            pltpu.VMEM((NODES, L4), jnp.float32),
            pltpu.VMEM((X // (2 * VS), 4 * PB, Z), jnp.float32),
            pltpu.VMEM((R, NV * 2 * VS), jnp.bfloat16),
            pltpu.VMEM((VS * E, R), jnp.bfloat16),
            pltpu.VMEM((NODES, 2 * VS * PB), jnp.bfloat16),
            dma((2, 6)), dma((2, 6)), dma((2, 6)), dma((2, 6)),
            dma((2, peers - 1)), dma((2, peers - 1)),
        ],
        compiler_params=pltpu.CompilerParams(
            collective_id=0, has_side_effects=True, vmem_limit_bytes=32 * 1024 * 1024
        ),
    )(
        *[
            pltpu.with_memory_space_constraint(x, pltpu.HBM)
            for x in (
                velocity, cells, projection, owner_index.reshape(1, NV), slot_element,
                element_cell,
            )
        ]
    )
    flow, stored = pl.pallas_call(
        finish,
        out_shape=(
            jax.ShapeDtypeStruct(velocity.shape, jnp.float32),
            jax.ShapeDtypeStruct((NODES, L4), jnp.float32),
        ),
        in_specs=[vmem] * 3,
        out_specs=(hbm, hbm),
        scratch_shapes=[pltpu.VMEM((NODES, L4), jnp.float32), dma((2,))],
        compiler_params=pltpu.CompilerParams(vmem_limit_bytes=16 * 1024 * 1024),
    )(flow, wave, perm)
    stored = stored.reshape(E, blocks, 4, L4).transpose(0, 2, 1, 3).reshape(acoustic.shape)
    return flow, stored


def solution(mesh):
    in_specs = (
        P(None, "gx", "gy", "gz"),
        P(("gx", "gy", "gz"), None, None),
        P(),
        P(("gx", "gy", "gz"), None),
        P(("gx", "gy", "gz"), None),
        P(("gx", "gy", "gz"), None),
    )
    out_specs = (P(None, "gx", "gy", "gz"), P(("gx", "gy", "gz"), None, None))
    return jax.shard_map(
        on_device, mesh=mesh, in_specs=in_specs, out_specs=out_specs, check_vma=False
    )
```

```python
import functools

import jax
import jax.numpy as jnp
import numpy as np
from jax import lax
from jax.experimental import pallas as pl
from jax.experimental.pallas import tpu as pltpu
from jax.sharding import PartitionSpec as P

VS = 4
ORDER = 7
EBX = 1
EBY = 2
EBZ = 16
K = ORDER + 1
FACE = K * K
NODES = K**3

HIGHEST = lax.Precision.HIGHEST
FLOW_STEP = 0.1
VISCOSITY = 0.05
WAVE_STEP = 0.02
SOURCE_GAIN = 25.0
MESH = pl.DeviceIdType.MESH


def legendre_table(points, order):
    columns = [points * 0.0 + 1.0, points]
    for degree in range(2, order + 1):
        columns.append(
            ((2 * degree - 1) * points * columns[degree - 1] - (degree - 1) * columns[degree - 2])
            / degree
        )
    return np.stack(columns, axis=1)


def lobatto_tables(order):
    point_count = order + 1
    points = -np.cos(np.pi * np.arange(point_count) / order)
    for newton_step in range(60):
        legendre = legendre_table(points, order)
        points = points - (points * legendre[:, order] - legendre[:, order - 1]) / (
            point_count * legendre[:, order]
        )
    legendre = legendre_table(points, order)
    highest = legendre[:, order]
    spacing = points[:, None] - points[None, :] + np.eye(point_count)
    derivative = highest[:, None] / (highest[None, :] * spacing)
    derivative = derivative * (1.0 - np.eye(point_count))
    derivative[0, 0] = -order * point_count / 4.0
    derivative[order, order] = order * point_count / 4.0
    return derivative


def iota(shape, axis):
    return lax.broadcasted_iota(jnp.int32, shape, axis)


def as_float(mask):
    return jnp.where(mask, 1.0, 0.0).astype(jnp.float32)


def to_column(row, count):
    eye = iota((count, count), 0) == iota((count, count), 1)
    return jnp.sum(jnp.where(eye, row, 0.0), axis=1, keepdims=True)


def spread_row(column, count, width, group):
    pick = iota((count, width), 0) == iota((count, width), 1) // group
    return jnp.sum(jnp.where(pick, column, 0.0), axis=0, keepdims=True)


def split(value):
    high = value.astype(jnp.bfloat16)
    low = (value - high.astype(jnp.float32)).astype(jnp.bfloat16)
    return high, low


def dot(a, b, contract=((1,), (0,)), precision=None):
    return lax.dot_general(
        a, b, (contract, ((), ())), preferred_element_type=jnp.float32, precision=precision
    )


def permutation(cell_row, elements):
    total = 4 * elements
    rows = iota((total, elements), 0)
    cell = jnp.sum(
        jnp.where(iota((total, elements), 1) == rows % elements, cell_row, 0.0),
        axis=1, keepdims=True,
    )
    r = iota((total, total), 0)
    goal = (r - r % elements).astype(jnp.float32) + cell
    return as_float(iota((total, total), 1).astype(jnp.float32) == goal).astype(jnp.bfloat16)


def swap(value, group, along, width):
    axis = value.ndim - 1
    total = 4 * width
    here = (1 + along) * width
    up = pltpu.roll(value, here, axis)
    down = up if 2 * here == total else pltpu.roll(value, total - here, axis)
    return jnp.where(group == 0, down, jnp.where(group == 1 + along, up, 0.0))


def derive(values, table):
    half = K // 2
    even = [values[j] + values[K - 1 - j] for j in range(half)]
    odd = [values[j] - values[K - 1 - j] for j in range(half)]
    result = [None] * K
    for a in range(half):
        first = sum(
            float(0.5 * (table[a, j] - table[a, K - 1 - j])) * odd[j] for j in range(half)
        )
        second = sum(
            float(0.5 * (table[a, j] + table[a, K - 1 - j])) * even[j] for j in range(half)
        )
        result[a] = first + second
        result[K - 1 - a] = first - second
    return result


def kernel(
    sizes,
    u_hbm, ac_hbm, proj_hbm, owner_hbm, slot_hbm, cell_hbm,
    u_out, ac_out, perm_out,
    u_in, ac_in, proj_in, owner_in, slot_in, cell_in, in_sems, flow, y_send, y_recv, z_send, z_recv, tr_send, tr_recv, vol_send, vol_recv,
    q_ref, acc, lhs, place, gather, proj_ref,
    v_ssem, v_rsem, t_ssem, t_rsem, p_ssem, p_rsem,
):
    nx, ny, nz, X, Y, Z, E, NV, cap = sizes
    peers = ny * nz
    gx, gy, gz = lax.axis_index("gx"), lax.axis_index("gy"), lax.axis_index("gz")
    me = gy * nz + gz
    across = [
        {"gx": lax.rem(gx + nx - 1, nx)}, {"gx": lax.rem(gx + 1, nx)},
        {"gy": lax.rem(gy + ny - 1, ny)}, {"gy": lax.rem(gy + 1, ny)},
        {"gz": lax.rem(gz + nz - 1, nz)}, {"gz": lax.rem(gz + 1, nz)},
    ]
    others = []
    for k in range(1, peers):
        p = lax.rem(me + k, peers)
        others.append((p, {"gy": lax.div(p, nz), "gz": lax.rem(p, nz)}))

    barrier = pltpu.get_barrier_semaphore()
    for target in across[:2] + [t for _, t in others]:
        pl.semaphore_signal(barrier, inc=1, device_id=target, device_id_type=MESH)

    sources = (u_hbm, cell_hbm, ac_hbm, owner_hbm, slot_hbm, proj_hbm)
    targets = (u_in, cell_in, ac_in, owner_in, slot_in, proj_in)
    loads = [
        pltpu.make_async_copy(src, dst, in_sems.at[i])
        for i, (src, dst) in enumerate(zip(sources, targets))
    ]
    for load in loads:
        load.start()

    lane = iota((Y, Z), 1)
    sub = iota((Y, Z), 0)

    def pack(t, x, values, carry):
        low, high = carry
        for c in range(3):
            at = c * X + x
            low = jnp.where(lane == at, pltpu.roll(values[c], at, 1), low)
            high = jnp.where(lane == at, pltpu.roll(values[c], at + 1, 1), high)
            y_send[t, 0, c, pl.ds(x, 1), :] = values[c][0:1]
            y_send[t, 1, c, pl.ds(x, 1), :] = values[c][Y - 1:Y]
        return low, high

    def fill(x, carry):
        values = [u_in[c, x] for c in range(3)]
        for c in range(3):
            flow[0, c, x + 1] = values[c]
        return pack(0, x, values, carry)

    blank = jnp.zeros((Y, Z), jnp.float32)

    def velocity_copies(t):
        result = []
        for f in range(6):
            s = f % 2
            if f < 2:
                src = flow.at[t, :, X if s else 1]
                dst = flow.at[t, :, 0 if s else X + 1]
            elif f < 4:
                src, dst = y_send.at[t, s], y_recv.at[t, 1 - s]
            else:
                src, dst = z_send.at[t, s], z_recv.at[t, 1 - s]
            result.append(
                pltpu.make_async_remote_copy(
                    src_ref=src, dst_ref=dst, send_sem=v_ssem.at[t, f],
                    recv_sem=v_rsem.at[t, f ^ 1], device_id=across[f], device_id_type=MESH,
                )
            )
        return result

    def trace_copies(t):
        return [
            pltpu.make_async_remote_copy(
                src_ref=tr_send.at[t, f], dst_ref=tr_recv.at[t, f ^ 1],
                send_sem=t_ssem.at[t, f], recv_sem=t_rsem.at[t, f ^ 1],
                device_id=across[f], device_id_type=MESH,
            )
            for f in range(6)
        ]

    def volume_copies(t):
        return [
            pltpu.make_async_remote_copy(
                src_ref=vol_send.at[t, p], dst_ref=vol_recv.at[t, me],
                send_sem=p_ssem.at[t, k], recv_sem=p_rsem.at[t, k],
                device_id=target, device_id_type=MESH,
            )
            for k, (p, target) in enumerate(others)
        ]

    loads[0].wait()
    low, high = lax.fori_loop(0, X, fill, (blank, blank), unroll=True)
    z_send[0, 0] = low
    z_send[0, 1] = high
    pl.semaphore_wait(barrier, peers + 1)

    def send_halos(t):
        copies = velocity_copies(t)
        for f in (0, 1, 4, 5, 2, 3):
            copies[f].start()

    send_halos(0)

    L4 = 4 * E
    loads[1].wait()
    loads[2].wait()
    cell_row = cell_in[...].astype(jnp.float32)
    perm = permutation(cell_row, E)
    perm_out[...] = perm
    blocks = NODES // L4
    stored = []
    for j in range(blocks):
        parts = [ac_in[pl.ds(4 * j + v, E, stride=4 * blocks), :] for v in range(4)]
        stored.append(jnp.concatenate(parts, axis=0).T)
    ah, al = split(jnp.concatenate(stored, axis=0))
    q_ref[...] = dot(
        jnp.concatenate([ah, al], axis=1), jnp.concatenate([perm, perm], axis=0)
    )

    def trace(f):
        a, s = f // 2, f % 2
        if a == 0:
            return q_ref[s * (K - 1) * FACE:s * (K - 1) * FACE + FACE, :]
        if a == 1:
            base = s * (K - 1) * K
            return jnp.concatenate(
                [q_ref[i * FACE + base:i * FACE + base + K, :] for i in range(K)], axis=0
            )
        return q_ref[pl.ds(s * (K - 1), FACE, stride=K), :]

    def send_traces(t):
        for f in range(6):
            tr_send[t, f] = trace(f).astype(jnp.bfloat16)
        for copy in trace_copies(t):
            copy.start()

    send_traces(0)

    cells = VS**3
    for load in loads[3:]:
        load.wait()
    own_row = owner_in[...].astype(jnp.float32)
    own = to_column(own_row, NV)
    matches = (own == own_row) & (iota((NV, NV), 1) < iota((NV, NV), 0))
    rank = jnp.sum(as_float(matches), axis=1, keepdims=True)
    slot_of = own * float(cap) + rank
    W = NV * 2 * VS
    R = peers * cap * VS
    slot_row = spread_row(slot_of, NV, W, 2 * VS)
    wl = iota((1, W), 1)
    goal = slot_row * float(VS) + ((wl % (2 * VS)) // 2).astype(jnp.float32)
    goal = jnp.where(wl % 2 == 0, goal, -1.0)
    place[...] = as_float(iota((R, W), 0).astype(jnp.float32) == goal).astype(jnp.bfloat16)

    slots = peers * cap
    slot_col = to_column(slot_in[...].astype(jnp.float32), slots)
    element_row = spread_row(slot_col, slots, R, VS)
    cell_col = to_column(cell_row, E)
    target_row = jnp.sum(
        jnp.where(iota((E, R), 0).astype(jnp.float32) == element_row, cell_col, 0.0),
        axis=0, keepdims=True,
    )
    goal = target_row + ((iota((1, R), 1) % VS) * E).astype(jnp.float32)
    gather[...] = as_float(iota((VS * E, R), 0).astype(jnp.float32) == goal).astype(jnp.bfloat16)

    PB = VS * Y
    pr = iota((VS * PB, cells), 0)
    pc = iota((VS * PB, cells), 1)
    source_cell = ((pr % PB) // Y * VS + (pr % Y) // 2) * VS + pr // PB
    select = as_float((source_cell == pc) & (pr % 2 == 0)) * (-WAVE_STEP * SOURCE_GAIN)
    arranged = dot(select, proj_in[...], precision=HIGHEST).T
    ph, plo = split(arranged)
    proj_ref[:, :VS * PB] = ph
    proj_ref[:, VS * PB:] = plo

    table = -WAVE_STEP * lobatto_tables(ORDER)
    group3 = iota((K, K, L4), 2) // E
    group2 = iota((FACE, L4), 1) // E
    sub3 = iota((K, K, L4), 1)

    def local_rates():
        factors = []
        subl = iota((K, L4), 0)
        for k in range(K):
            factor = jnp.zeros((K, L4), jnp.float32)
            for c in range(K):
                factor = jnp.where(subl == c, float(table[c, (c - k) % K]), factor)
            factors.append(factor)

        def first(i, carry):
            at = pl.multiple_of(i * FACE, FACE)
            x = q_ref[pl.ds(at, FACE), :].reshape(K, K, L4)
            total = x
            s2 = swap(x, group3, 2, E)
            for k in range(K):
                rolled = s2 if k == 0 else pltpu.roll(s2, k, 1)
                total = total + factors[k][None] * rolled
            s1 = swap(x, group3, 1, E)
            parts = derive([s1[j] for j in range(K)], table)
            total = total + jnp.stack(parts)
            acc[pl.ds(at, FACE), :] = total.reshape(FACE, L4)
            return carry

        lax.fori_loop(0, K, first, 0, unroll=True)

        def second(i, carry):
            ats = [pl.multiple_of(a * FACE + i * K, K) for a in range(K)]
            x = jnp.stack([q_ref[pl.ds(at, K), :] for at in ats])
            s0 = swap(x, group3, 0, E)
            parts = derive([s0[j] for j in range(K)], table)
            for at, part in zip(ats, parts):
                acc[pl.ds(at, K), :] += part
            return carry

        lax.fori_loop(0, K, second, 0, unroll=True)

    lane2 = iota((FACE, L4), 1)
    y_of = (lane2 % E) // EBZ
    z_of = lane2 % EBZ
    scale = WAVE_STEP * 0.5 * ORDER * (ORDER + 1) / 2.0

    def add_flux(t):
        for f in range(6):
            a, s = f // 2, f % 2
            inner = trace(f)
            other = tr_recv[t, f].astype(jnp.float32)
            if a == 0:
                outer = other
            elif a == 1:
                mine = trace(f ^ 1)
                edge = 0 if s else EBY - 1
                mixed = jnp.where(y_of == edge, other, mine)
                near = EBZ if s == 0 else L4 - EBZ
                wrap = (L4 - (EBY - 1) * EBZ) if s == 0 else (EBY - 1) * EBZ
                outer = jnp.where(
                    y_of == (EBY - 1 if s else 0),
                    pltpu.roll(mixed, wrap, 1), pltpu.roll(mixed, near, 1),
                )
            else:
                mine = trace(f ^ 1)
                edge = 0 if s else EBZ - 1
                mixed = jnp.where(z_of == edge, other, mine)
                near = 1 if s == 0 else L4 - 1
                wrap = (L4 - (EBZ - 1)) if s == 0 else EBZ - 1
                outer = jnp.where(
                    z_of == (EBZ - 1 if s else 0),
                    pltpu.roll(mixed, wrap, 1), pltpu.roll(mixed, near, 1),
                )
            jump = inner - outer
            turned = swap(jump, group2, a, E)
            flux = scale * ((turned if s else -turned) - jump)
            if a == 0:
                base = s * (K - 1) * FACE
                acc[base:base + FACE, :] += flux
            elif a == 1:
                base = s * (K - 1) * K
                for i in range(K):
                    at = i * FACE + base
                    acc[at:at + K, :] += flux[i * K:(i + 1) * K]
            else:
                where = pl.ds(s * (K - 1), FACE, stride=K)
                acc[where, :] = acc[where, :] + flux

    def flow_step(t):
        z_low = z_recv[t, 0]
        z_high = z_recv[t, 1]

        def column(x, carry):
            centre = [flow[t, c, x + 1] for c in range(3)]
            below, above = [], []
            for c in range(3):
                at = c * X + x
                u = centre[c]
                pair = (flow[t, c, x], flow[t, c, x + 2])
                y_low = y_recv[t, 0, c, pl.ds(x, 1), :]
                y_high = y_recv[t, 1, c, pl.ds(x, 1), :]
                ym = jnp.where(sub == 0, y_low, pltpu.roll(u, 1, 0))
                yp = jnp.where(sub == Y - 1, y_high, pltpu.roll(u, Y - 1, 0))
                zm = jnp.where(
                    lane == 0, pltpu.roll(z_low, lax.rem(Z - at, Z), 1), pltpu.roll(u, 1, 1)
                )
                zp = jnp.where(
                    lane == Z - 1, pltpu.roll(z_high, Z - 1 - at, 1), pltpu.roll(u, Z - 1, 1)
                )
                below.append((pair[0], ym, zm))
                above.append((pair[1], yp, zp))
            slope = [[0.5 * (above[c][a] - below[c][a]) for c in range(3)] for a in range(3)]
            updated = []
            for c in range(3):
                rate = VISCOSITY * (
                    (above[c][0] + below[c][0])
                    + (above[c][1] + below[c][1])
                    + (above[c][2] + below[c][2])
                    - 6.0 * centre[c]
                )
                for a in range(3):
                    rate = rate - centre[a] * slope[a][c]
                updated.append(centre[c] + FLOW_STEP * rate)
            w = [
                slope[1][2] - slope[2][1], slope[2][0] - slope[0][2], slope[0][1] - slope[1][0]
            ]
            lamb = [
                w[1] * centre[2] - w[2] * centre[1],
                w[2] * centre[0] - w[0] * centre[2],
                w[0] * centre[1] - w[1] * centre[0],
            ]
            for c in range(3):
                flow[t + 1, c, x + 1] = updated[c]
                u_out[c, x] = updated[c]
            carry = pack(t + 1, x, updated, carry)
            return lamb, carry

        def couple(i, carry):
            first, carry = column(2 * i, carry)
            second, carry = column(2 * i + 1, carry)
            block = lax.div(i, VS)
            row = lax.rem(i, VS)
            for c in range(3):
                total = first[c] + second[c]
                total = total + pltpu.roll(total, Y - 1, 0)
                total = total + pltpu.roll(total, Z - 1, 1)
                at = pl.multiple_of(c * PB + row * Y, Y)
                lhs[block, pl.ds(at, Y), :] = 0.125 * total
            return carry

        carry = lax.fori_loop(0, X // 2, couple, (blank, blank), unroll=True)
        z_send[t + 1, 0] = carry[0]
        z_send[t + 1, 1] = carry[1]

    def send_volumes(t):
        wide = jnp.concatenate([lhs[i] for i in range(X // (2 * VS))], axis=1)
        sent = dot(place[...], wide.astype(jnp.bfloat16), ((1,), (1,)))
        vol_send[t] = sent.astype(vol_send.dtype).reshape(peers, cap * VS, 4 * PB)
        for copy in volume_copies(t):
            copy.start()
        vol_recv[t, me] = vol_send[t, me]

    def add_source(t):
        received = vol_recv[t].reshape(R, 4 * PB).astype(jnp.bfloat16)
        summed = dot(gather[...], received).T
        group = iota((PB, L4), 1) // E
        blocks = []
        for c in range(VS):
            block = jnp.zeros((PB, L4), jnp.float32)
            for v in range(3):
                part = summed[v * PB:(v + 1) * PB]
                shift = ((1 + v - c) * E) % L4
                if shift:
                    part = pltpu.roll(part, shift, 1)
                block = jnp.where(group == 1 + v, part, block)
            blocks.append(block)
        bh, bl = split(jnp.concatenate(blocks, axis=0))
        source = dot(proj_ref[...], jnp.concatenate([bh, bh], axis=0))
        source = source + dot(proj_ref[:, :VS * PB], bl)
        acc[...] = acc[...] + source

    lhs[...] = jnp.zeros_like(lhs)

    def arrive(copies):
        for copy in copies:
            copy.wait_recv()

    def step(t, carry):
        arrive(velocity_copies(t))
        flow_step(t)
        send_volumes(t)

        @pl.when(t == 0)
        def _():
            send_halos(1)

        @pl.when(t == 1)
        def _():
            arrive(volume_copies(0))
            add_source(0)
            q_ref[...] = acc[...]
            send_traces(1)

        local_rates()

        @pl.when(t == 1)
        def _():
            arrive(volume_copies(1))
            add_source(1)

        arrive(trace_copies(t))
        add_flux(t)
        return carry

    lax.fori_loop(0, 2, step, 0)
    ac_out[...] = acc[...]

    def leave(t, carry):
        for copies in (velocity_copies(t), trace_copies(t), volume_copies(t)):
            for copy in copies:
                copy.wait_send()
        return carry

    lax.fori_loop(0, 2, leave, 0)


def finish(u_in, q_in, perm_in, u_hbm, ac_hbm, ac_out, sems):
    flow_copy = pltpu.make_async_copy(u_in, u_hbm, sems.at[0])
    flow_copy.start()
    nodes, total = q_in.shape
    E = total // 4
    perm = perm_in[...]
    high, low = split(q_in[...])
    stored = dot(
        jnp.concatenate([perm, perm], axis=1), jnp.concatenate([high, low], axis=1), ((1,), (1,))
    )
    blocks = nodes // total
    for j in range(blocks):
        for v in range(4):
            ac_out[pl.ds(4 * j + v, E, stride=4 * blocks), :] = stored[
                v * E:(v + 1) * E, j * total:(j + 1) * total
            ]
    wave_copy = pltpu.make_async_copy(ac_out, ac_hbm, sems.at[1])
    wave_copy.start()
    flow_copy.wait()
    wave_copy.wait()


def on_device(velocity, acoustic, projection, owner_index, slot_element, element_cell):
    nx, ny, nz = lax.axis_size("gx"), lax.axis_size("gy"), lax.axis_size("gz")
    _, X, Y, Z = velocity.shape
    E = acoustic.shape[0]
    NV = owner_index.shape[0]
    peers = ny * nz
    cap = slot_element.shape[1] // peers
    sizes = (nx, ny, nz, X, Y, Z, E, NV, cap)
    R = peers * cap * VS
    PB = VS * Y
    L4 = 4 * E
    travel = jnp.bfloat16 if (cap * VS) % 16 == 0 else jnp.float32
    vmem = pl.BlockSpec(memory_space=pltpu.VMEM)
    hbm = pl.BlockSpec(memory_space=pltpu.HBM)
    dma = pltpu.SemaphoreType.DMA
    blocks = NODES // L4
    cells = acoustic.reshape(E, 4, blocks, L4).transpose(0, 2, 1, 3).reshape(NODES, L4)
    flow, wave, perm = pl.pallas_call(
        functools.partial(kernel, sizes),
        out_shape=(
            jax.ShapeDtypeStruct(velocity.shape, jnp.float32),
            jax.ShapeDtypeStruct((NODES, L4), jnp.float32),
            jax.ShapeDtypeStruct((L4, L4), jnp.bfloat16),
        ),
        in_specs=[hbm] * 6,
        out_specs=(vmem, vmem, vmem),
        scratch_shapes=[
            pltpu.VMEM(velocity.shape, jnp.float32),
            pltpu.VMEM((NODES, L4), jnp.float32),
            pltpu.VMEM(projection.shape, jnp.float32),
            pltpu.VMEM((1, NV), jnp.int32),
            pltpu.VMEM(slot_element.shape, jnp.int32),
            pltpu.VMEM(element_cell.shape, jnp.int32),
            dma((6,)),
            pltpu.VMEM((3, 3, X + 2, Y, Z), jnp.float32),
            pltpu.VMEM((3, 2, 3, X, Z), jnp.float32),
            pltpu.VMEM((2, 2, 3, X, Z), jnp.float32),
            pltpu.VMEM((3, 2, Y, Z), jnp.float32),
            pltpu.VMEM((2, 2, Y, Z), jnp.float32),
            pltpu.VMEM((2, 6, FACE, L4), jnp.bfloat16),
            pltpu.VMEM((2, 6, FACE, L4), jnp.bfloat16),
            pltpu.VMEM((2, peers, cap * VS, 4 * PB), travel),
            pltpu.VMEM((2, peers, cap * VS, 4 * PB), travel),
            pltpu.VMEM((NODES, L4), jnp.float32),
            pltpu.VMEM((NODES, L4), jnp.float32),
            pltpu.VMEM((X // (2 * VS), 4 * PB, Z), jnp.float32),
            pltpu.VMEM((R, NV * 2 * VS), jnp.bfloat16),
            pltpu.VMEM((VS * E, R), jnp.bfloat16),
            pltpu.VMEM((NODES, 2 * VS * PB), jnp.bfloat16),
            dma((2, 6)), dma((2, 6)), dma((2, 6)), dma((2, 6)),
            dma((2, peers - 1)), dma((2, peers - 1)),
        ],
        compiler_params=pltpu.CompilerParams(
            collective_id=0, has_side_effects=True, vmem_limit_bytes=32 * 1024 * 1024
        ),
    )(
        *[
            pltpu.with_memory_space_constraint(x, pltpu.HBM)
            for x in (
                velocity, cells, projection, owner_index.reshape(1, NV), slot_element,
                element_cell,
            )
        ]
    )
    flow, stored = pl.pallas_call(
        finish,
        out_shape=(
            jax.ShapeDtypeStruct(velocity.shape, jnp.float32),
            jax.ShapeDtypeStruct((NODES, L4), jnp.float32),
        ),
        in_specs=[vmem] * 3,
        out_specs=(hbm, hbm),
        scratch_shapes=[pltpu.VMEM((NODES, L4), jnp.float32), dma((2,))],
        compiler_params=pltpu.CompilerParams(vmem_limit_bytes=16 * 1024 * 1024),
    )(flow, wave, perm)
    stored = stored.reshape(E, blocks, 4, L4).transpose(0, 2, 1, 3).reshape(acoustic.shape)
    return flow, stored


def solution(mesh):
    in_specs = (
        P(None, "gx", "gy", "gz"),
        P(("gx", "gy", "gz"), None, None),
        P(),
        P(("gx", "gy", "gz"), None),
        P(("gx", "gy", "gz"), None),
        P(("gx", "gy", "gz"), None),
    )
    out_specs = (P(None, "gx", "gy", "gz"), P(("gx", "gy", "gz"), None, None))
    return jax.shard_map(
        on_device, mesh=mesh, in_specs=in_specs, out_specs=out_specs, check_vma=False
    )
```

```python
import functools

import jax
import jax.numpy as jnp
import numpy as np
from jax import lax
from jax.experimental import pallas as pl
from jax.experimental.pallas import tpu as pltpu
from jax.sharding import PartitionSpec as P

VS = 4
ORDER = 7
EBX = 1
EBY = 2
EBZ = 16
K = ORDER + 1
FACE = K * K
NODES = K**3

HIGHEST = lax.Precision.HIGHEST
FLOW_STEP = 0.1
VISCOSITY = 0.05
WAVE_STEP = 0.02
SOURCE_GAIN = 25.0
MESH = pl.DeviceIdType.MESH


def legendre_table(points, order):
    columns = [points * 0.0 + 1.0, points]
    for degree in range(2, order + 1):
        columns.append(
            ((2 * degree - 1) * points * columns[degree - 1] - (degree - 1) * columns[degree - 2])
            / degree
        )
    return np.stack(columns, axis=1)


def lobatto_tables(order):
    point_count = order + 1
    points = -np.cos(np.pi * np.arange(point_count) / order)
    for newton_step in range(60):
        legendre = legendre_table(points, order)
        points = points - (points * legendre[:, order] - legendre[:, order - 1]) / (
            point_count * legendre[:, order]
        )
    legendre = legendre_table(points, order)
    highest = legendre[:, order]
    spacing = points[:, None] - points[None, :] + np.eye(point_count)
    derivative = highest[:, None] / (highest[None, :] * spacing)
    derivative = derivative * (1.0 - np.eye(point_count))
    derivative[0, 0] = -order * point_count / 4.0
    derivative[order, order] = order * point_count / 4.0
    return derivative


def iota(shape, axis):
    return lax.broadcasted_iota(jnp.int32, shape, axis)


def as_float(mask):
    return jnp.where(mask, 1.0, 0.0).astype(jnp.float32)


def to_column(row, count):
    eye = iota((count, count), 0) == iota((count, count), 1)
    return jnp.sum(jnp.where(eye, row, 0.0), axis=1, keepdims=True)


def spread_row(column, count, width, group):
    pick = iota((count, width), 0) == iota((count, width), 1) // group
    return jnp.sum(jnp.where(pick, column, 0.0), axis=0, keepdims=True)


def split(value):
    high = value.astype(jnp.bfloat16)
    low = (value - high.astype(jnp.float32)).astype(jnp.bfloat16)
    return high, low


def dot(a, b, contract=((1,), (0,)), precision=None):
    return lax.dot_general(
        a, b, (contract, ((), ())), preferred_element_type=jnp.float32, precision=precision
    )


def permutation(cell_row, elements):
    total = 4 * elements
    rows = iota((total, elements), 0)
    cell = jnp.sum(
        jnp.where(iota((total, elements), 1) == rows % elements, cell_row, 0.0),
        axis=1, keepdims=True,
    )
    r = iota((total, total), 0)
    goal = (r - r % elements).astype(jnp.float32) + cell
    return as_float(iota((total, total), 1).astype(jnp.float32) == goal).astype(jnp.bfloat16)


def swap(value, group, along, width):
    axis = value.ndim - 1
    total = 4 * width
    here = (1 + along) * width
    up = pltpu.roll(value, here, axis)
    down = up if 2 * here == total else pltpu.roll(value, total - here, axis)
    return jnp.where(group == 0, down, jnp.where(group == 1 + along, up, 0.0))


def derive(values, table):
    half = K // 2
    even = [values[j] + values[K - 1 - j] for j in range(half)]
    odd = [values[j] - values[K - 1 - j] for j in range(half)]
    result = [None] * K
    for a in range(half):
        first = sum(
            float(0.5 * (table[a, j] - table[a, K - 1 - j])) * odd[j] for j in range(half)
        )
        second = sum(
            float(0.5 * (table[a, j] + table[a, K - 1 - j])) * even[j] for j in range(half)
        )
        result[a] = first + second
        result[K - 1 - a] = first - second
    return result


def kernel(
    sizes,
    u_hbm, ac_hbm, proj_hbm, owner_hbm, slot_hbm, cell_hbm,
    u_out, ac_out, perm_out,
    u_in, ac_in, proj_in, owner_in, slot_in, cell_in, in_sems, flow, y_send, y_recv, z_send, z_recv, tr_send, tr_recv, vol_send, vol_recv,
    q_ref, acc, lhs, place, gather, proj_ref, summed, spare,
    v_ssem, v_rsem, t_ssem, t_rsem, p_ssem, p_rsem,
):
    nx, ny, nz, X, Y, Z, E, NV, cap = sizes
    peers = ny * nz
    gx, gy, gz = lax.axis_index("gx"), lax.axis_index("gy"), lax.axis_index("gz")
    me = gy * nz + gz
    across = [
        {"gx": lax.rem(gx + nx - 1, nx)}, {"gx": lax.rem(gx + 1, nx)},
        {"gy": lax.rem(gy + ny - 1, ny)}, {"gy": lax.rem(gy + 1, ny)},
        {"gz": lax.rem(gz + nz - 1, nz)}, {"gz": lax.rem(gz + 1, nz)},
    ]
    others = []
    for k in range(1, peers):
        p = lax.rem(me + k, peers)
        others.append((p, {"gy": lax.div(p, nz), "gz": lax.rem(p, nz)}))

    barrier = pltpu.get_barrier_semaphore()
    for target in across[:2] + [t for _, t in others]:
        pl.semaphore_signal(barrier, inc=1, device_id=target, device_id_type=MESH)

    sources = (u_hbm, owner_hbm, cell_hbm, ac_hbm, slot_hbm, proj_hbm)
    targets = (u_in, owner_in, cell_in, ac_in, slot_in, proj_in)
    loads = [
        pltpu.make_async_copy(src, dst, in_sems.at[i])
        for i, (src, dst) in enumerate(zip(sources, targets))
    ]
    for load in loads:
        load.start()

    lane = iota((Y, Z), 1)
    sub = iota((Y, Z), 0)

    def pack(t, x, values, carry):
        low, high = carry
        for c in range(3):
            at = c * X + x
            low = jnp.where(lane == at, pltpu.roll(values[c], at, 1), low)
            high = jnp.where(lane == at, pltpu.roll(values[c], at + 1, 1), high)
            y_send[t, 0, c, pl.ds(x, 1), :] = values[c][0:1]
            y_send[t, 1, c, pl.ds(x, 1), :] = values[c][Y - 1:Y]
        return low, high

    def fill(x, carry):
        values = [u_in[c, x] for c in range(3)]
        for c in range(3):
            flow[0, c, x + 1] = values[c]
        return pack(0, x, values, carry)

    blank = jnp.zeros((Y, Z), jnp.float32)

    def velocity_copies(t):
        result = []
        for f in range(6):
            s = f % 2
            if f < 2:
                src = flow.at[t, :, X if s else 1]
                dst = flow.at[t, :, 0 if s else X + 1]
            elif f < 4:
                src, dst = y_send.at[t, s], y_recv.at[t, 1 - s]
            else:
                src, dst = z_send.at[t, s], z_recv.at[t, 1 - s]
            result.append(
                pltpu.make_async_remote_copy(
                    src_ref=src, dst_ref=dst, send_sem=v_ssem.at[t, f],
                    recv_sem=v_rsem.at[t, f ^ 1], device_id=across[f], device_id_type=MESH,
                )
            )
        return result

    def trace_copies(t):
        return [
            pltpu.make_async_remote_copy(
                src_ref=tr_send.at[t, f], dst_ref=tr_recv.at[t, f ^ 1],
                send_sem=t_ssem.at[t, f], recv_sem=t_rsem.at[t, f ^ 1],
                device_id=across[f], device_id_type=MESH,
            )
            for f in range(6)
        ]

    def volume_copies(t):
        return [
            pltpu.make_async_remote_copy(
                src_ref=vol_send.at[t, p], dst_ref=vol_recv.at[t, me],
                send_sem=p_ssem.at[t, k], recv_sem=p_rsem.at[t, k],
                device_id=target, device_id_type=MESH,
            )
            for k, (p, target) in enumerate(others)
        ]

    loads[0].wait()
    low, high = lax.fori_loop(0, X, fill, (blank, blank), unroll=True)
    z_send[0, 0] = low
    z_send[0, 1] = high
    pl.semaphore_wait(barrier, peers + 1)

    def send_halos(t):
        copies = velocity_copies(t)
        for f in (0, 1, 4, 5, 2, 3):
            copies[f].start()

    send_halos(0)

    for load in loads[1:4]:
        load.wait()
    own_row = owner_in[...].astype(jnp.float32)
    own = to_column(own_row, NV)
    matches = (own == own_row) & (iota((NV, NV), 1) < iota((NV, NV), 0))
    rank = jnp.sum(as_float(matches), axis=1, keepdims=True)
    slot_of = own * float(cap) + rank
    W = NV * 2 * VS
    slot_row = spread_row(slot_of, NV, W, 2 * VS)
    wl = iota((1, W), 1)
    goal = slot_row * float(VS) + ((wl % (2 * VS)) // 2).astype(jnp.float32)
    goal = jnp.where(wl % 2 == 0, goal, -1.0)
    place[...] = as_float(
        iota((peers * cap * VS, W), 0).astype(jnp.float32) == goal
    ).astype(jnp.bfloat16)

    L4 = 4 * E
    cell_row = cell_in[...].astype(jnp.float32)
    perm = permutation(cell_row, E)
    perm_out[...] = perm
    blocks = NODES // L4
    stored = []
    for j in range(blocks):
        parts = [ac_in[pl.ds(4 * j + v, E, stride=4 * blocks), :] for v in range(4)]
        stored.append(jnp.concatenate(parts, axis=0).T)
    ah, al = split(jnp.concatenate(stored, axis=0))
    q_ref[...] = dot(
        jnp.concatenate([ah, al], axis=1), jnp.concatenate([perm, perm], axis=0)
    )

    def trace(f):
        a, s = f // 2, f % 2
        if a == 0:
            return q_ref[s * (K - 1) * FACE:s * (K - 1) * FACE + FACE, :]
        if a == 1:
            base = s * (K - 1) * K
            return jnp.concatenate(
                [q_ref[i * FACE + base:i * FACE + base + K, :] for i in range(K)], axis=0
            )
        return q_ref[pl.ds(s * (K - 1), FACE, stride=K), :]

    def send_traces(t):
        for f in range(6):
            tr_send[t, f] = trace(f).astype(jnp.bfloat16)
        for copy in trace_copies(t):
            copy.start()

    send_traces(0)

    R = peers * cap * VS
    PB = VS * Y
    cells = VS**3

    def source_tables():
        slots = peers * cap
        slot_col = to_column(slot_in[...].astype(jnp.float32), slots)
        element_row = spread_row(slot_col, slots, R, VS)
        cell_col = to_column(cell_row, E)
        target_row = jnp.sum(
            jnp.where(iota((E, R), 0).astype(jnp.float32) == element_row, cell_col, 0.0),
            axis=0, keepdims=True,
        )
        goal = target_row + ((iota((1, R), 1) % VS) * E).astype(jnp.float32)
        gather[...] = as_float(
            iota((VS * E, R), 0).astype(jnp.float32) == goal
        ).astype(jnp.bfloat16)
        blocks = NODES // L4
        for j in range(blocks):
            spare[j * cells:(j + 1) * cells, :] = proj_in[:, j * L4:(j + 1) * L4]
        rows = [
            jnp.concatenate(
                [spare[pl.ds(j * cells + c, VS * VS, stride=VS), :] for j in range(blocks)], axis=1
            )
            for c in range(VS)
        ]
        scaled = (-WAVE_STEP * SOURCE_GAIN) * jnp.concatenate(rows, axis=0)
        high, low = split(scaled)
        both = jnp.concatenate([high.astype(jnp.float32), low.astype(jnp.float32)], axis=0)
        turned = both.T.astype(jnp.bfloat16)
        proj_ref[...] = jnp.concatenate([turned, turned], axis=1)

    table = -WAVE_STEP * lobatto_tables(ORDER)
    group3 = iota((K, K, L4), 2) // E
    group2 = iota((FACE, L4), 1) // E
    sub3 = iota((K, K, L4), 1)

    def local_rates():
        factors = []
        subl = iota((K, L4), 0)
        for k in range(K):
            factor = jnp.zeros((K, L4), jnp.float32)
            for c in range(K):
                factor = jnp.where(subl == c, float(table[c, (c - k) % K]), factor)
            factors.append(factor)

        def first(i, carry):
            at = pl.multiple_of(i * FACE, FACE)
            x = q_ref[pl.ds(at, FACE), :].reshape(K, K, L4)
            total = x
            s2 = swap(x, group3, 2, E)
            for k in range(K):
                rolled = s2 if k == 0 else pltpu.roll(s2, k, 1)
                total = total + factors[k][None] * rolled
            s1 = swap(x, group3, 1, E)
            parts = derive([s1[j] for j in range(K)], table)
            total = total + jnp.stack(parts)
            acc[pl.ds(at, FACE), :] = total.reshape(FACE, L4)
            return carry

        lax.fori_loop(0, K, first, 0, unroll=True)

        def second(i, carry):
            ats = [pl.multiple_of(a * FACE + i * K, K) for a in range(K)]
            x = jnp.stack([q_ref[pl.ds(at, K), :] for at in ats])
            s0 = swap(x, group3, 0, E)
            parts = derive([s0[j] for j in range(K)], table)
            for at, part in zip(ats, parts):
                acc[pl.ds(at, K), :] += part
            return carry

        lax.fori_loop(0, K, second, 0, unroll=True)

    lane2 = iota((FACE, L4), 1)
    y_of = (lane2 % E) // EBZ
    z_of = lane2 % EBZ
    scale = WAVE_STEP * 0.5 * ORDER * (ORDER + 1) / 2.0

    def add_flux(t):
        for f in range(6):
            a, s = f // 2, f % 2
            inner = trace(f)
            other = tr_recv[t, f].astype(jnp.float32)
            if a == 0:
                outer = other
            elif a == 1:
                mine = trace(f ^ 1)
                edge = 0 if s else EBY - 1
                mixed = jnp.where(y_of == edge, other, mine)
                near = EBZ if s == 0 else L4 - EBZ
                wrap = (L4 - (EBY - 1) * EBZ) if s == 0 else (EBY - 1) * EBZ
                outer = jnp.where(
                    y_of == (EBY - 1 if s else 0),
                    pltpu.roll(mixed, wrap, 1), pltpu.roll(mixed, near, 1),
                )
            else:
                mine = trace(f ^ 1)
                edge = 0 if s else EBZ - 1
                mixed = jnp.where(z_of == edge, other, mine)
                near = 1 if s == 0 else L4 - 1
                wrap = (L4 - (EBZ - 1)) if s == 0 else EBZ - 1
                outer = jnp.where(
                    z_of == (EBZ - 1 if s else 0),
                    pltpu.roll(mixed, wrap, 1), pltpu.roll(mixed, near, 1),
                )
            jump = inner - outer
            turned = swap(jump, group2, a, E)
            flux = scale * ((turned if s else -turned) - jump)
            if a == 0:
                base = s * (K - 1) * FACE
                acc[base:base + FACE, :] += flux
            elif a == 1:
                base = s * (K - 1) * K
                for i in range(K):
                    at = i * FACE + base
                    acc[at:at + K, :] += flux[i * K:(i + 1) * K]
            else:
                where = pl.ds(s * (K - 1), FACE, stride=K)
                acc[where, :] = acc[where, :] + flux

    def flow_step(t):
        z_low = z_recv[t, 0]
        z_high = z_recv[t, 1]

        def column(x, carry):
            centre = [flow[t, c, x + 1] for c in range(3)]
            below, above = [], []
            for c in range(3):
                at = c * X + x
                u = centre[c]
                pair = (flow[t, c, x], flow[t, c, x + 2])
                y_low = y_recv[t, 0, c, pl.ds(x, 1), :]
                y_high = y_recv[t, 1, c, pl.ds(x, 1), :]
                ym = jnp.where(sub == 0, y_low, pltpu.roll(u, 1, 0))
                yp = jnp.where(sub == Y - 1, y_high, pltpu.roll(u, Y - 1, 0))
                zm = jnp.where(
                    lane == 0, pltpu.roll(z_low, lax.rem(Z - at, Z), 1), pltpu.roll(u, 1, 1)
                )
                zp = jnp.where(
                    lane == Z - 1, pltpu.roll(z_high, Z - 1 - at, 1), pltpu.roll(u, Z - 1, 1)
                )
                below.append((pair[0], ym, zm))
                above.append((pair[1], yp, zp))
            slope = [[0.5 * (above[c][a] - below[c][a]) for c in range(3)] for a in range(3)]
            updated = []
            for c in range(3):
                rate = VISCOSITY * (
                    (above[c][0] + below[c][0])
                    + (above[c][1] + below[c][1])
                    + (above[c][2] + below[c][2])
                    - 6.0 * centre[c]
                )
                for a in range(3):
                    rate = rate - centre[a] * slope[a][c]
                updated.append(centre[c] + FLOW_STEP * rate)
            w = [
                slope[1][2] - slope[2][1], slope[2][0] - slope[0][2], slope[0][1] - slope[1][0]
            ]
            lamb = [
                w[1] * centre[2] - w[2] * centre[1],
                w[2] * centre[0] - w[0] * centre[2],
                w[0] * centre[1] - w[1] * centre[0],
            ]
            for c in range(3):
                flow[t + 1, c, x + 1] = updated[c]
                u_out[c, x] = updated[c]
            carry = pack(t + 1, x, updated, carry)
            return lamb, carry

        def couple(i, carry):
            first, carry = column(2 * i, carry)
            second, carry = column(2 * i + 1, carry)
            block = lax.div(i, VS)
            row = lax.rem(i, VS)
            for c in range(3):
                total = first[c] + second[c]
                total = total + pltpu.roll(total, Y - 1, 0)
                total = total + pltpu.roll(total, Z - 1, 1)
                at = pl.multiple_of(c * PB + row * Y, Y)
                lhs[block, pl.ds(at, Y), :] = 0.125 * total
            return carry

        carry = lax.fori_loop(0, X // 2, couple, (blank, blank), unroll=True)
        z_send[t + 1, 0] = carry[0]
        z_send[t + 1, 1] = carry[1]

    def send_volumes(t):
        wide = jnp.concatenate([lhs[i] for i in range(X // (2 * VS))], axis=1)
        sent = dot(place[...], wide.astype(jnp.bfloat16), ((1,), (1,)))
        vol_send[t] = sent.astype(vol_send.dtype).reshape(peers, cap * VS, 4 * PB)
        for copy in volume_copies(t):
            copy.start()
        vol_recv[t, me] = vol_send[t, me]

    def add_source(t):
        received = vol_recv[t].reshape(R, 4 * PB).astype(jnp.bfloat16)
        summed[...] = dot(gather[...], received).T
        count = VS * VS
        group = iota((count, L4), 1) // E
        parts = [summed[pl.ds(v * PB, count, stride=2), :] for v in range(3)]
        blocks = []
        for c in range(VS):
            block = jnp.zeros((count, L4), jnp.float32)
            for v in range(3):
                shift = ((1 + v - c) * E) % L4
                part = pltpu.roll(parts[v], shift, 1) if shift else parts[v]
                block = jnp.where(group == 1 + v, part, block)
            blocks.append(block)
        high, low = split(jnp.concatenate(blocks, axis=0))
        acc[...] += dot(proj_ref[...], jnp.concatenate([high, high, low, low], axis=0))

    lhs[...] = jnp.zeros_like(lhs)

    def arrive(copies):
        for copy in copies:
            copy.wait_recv()

    def step(t, carry):
        arrive(velocity_copies(t))
        flow_step(t)

        @pl.when(t == 0)
        def _():
            send_halos(1)

        send_volumes(t)

        @pl.when(t == 0)
        def _():
            for load in loads[4:]:
                load.wait()
            source_tables()

        @pl.when(t == 1)
        def _():
            arrive(volume_copies(0))
            add_source(0)
            q_ref[...] = acc[...]
            send_traces(1)

        local_rates()

        @pl.when(t == 1)
        def _():
            arrive(volume_copies(1))
            add_source(1)

        arrive(trace_copies(t))
        add_flux(t)
        return carry

    lax.fori_loop(0, 2, step, 0)
    ac_out[...] = acc[...]

    def leave(t, carry):
        for copies in (velocity_copies(t), trace_copies(t), volume_copies(t)):
            for copy in copies:
                copy.wait_send()
        return carry

    lax.fori_loop(0, 2, leave, 0)


def finish(u_in, q_in, perm_in, u_hbm, ac_hbm, ac_out, sems):
    flow_copy = pltpu.make_async_copy(u_in, u_hbm, sems.at[0])
    flow_copy.start()
    nodes, total = q_in.shape
    E = total // 4
    perm = perm_in[...]
    high, low = split(q_in[...])
    stored = dot(
        jnp.concatenate([perm, perm], axis=1), jnp.concatenate([high, low], axis=1), ((1,), (1,))
    )
    blocks = nodes // total
    for j in range(blocks):
        for v in range(4):
            ac_out[pl.ds(4 * j + v, E, stride=4 * blocks), :] = stored[
                v * E:(v + 1) * E, j * total:(j + 1) * total
            ]
    wave_copy = pltpu.make_async_copy(ac_out, ac_hbm, sems.at[1])
    wave_copy.start()
    flow_copy.wait()
    wave_copy.wait()


def on_device(velocity, acoustic, projection, owner_index, slot_element, element_cell):
    nx, ny, nz = lax.axis_size("gx"), lax.axis_size("gy"), lax.axis_size("gz")
    _, X, Y, Z = velocity.shape
    E = acoustic.shape[0]
    NV = owner_index.shape[0]
    peers = ny * nz
    cap = slot_element.shape[1] // peers
    sizes = (nx, ny, nz, X, Y, Z, E, NV, cap)
    R = peers * cap * VS
    PB = VS * Y
    L4 = 4 * E
    blocks = NODES // L4
    travel = jnp.bfloat16 if (cap * VS) % 16 == 0 else jnp.float32
    vmem = pl.BlockSpec(memory_space=pltpu.VMEM)
    hbm = pl.BlockSpec(memory_space=pltpu.HBM)
    dma = pltpu.SemaphoreType.DMA
    cells = acoustic.reshape(E, 4, blocks, L4).transpose(0, 2, 1, 3).reshape(NODES, L4)
    flow, wave, perm = pl.pallas_call(
        functools.partial(kernel, sizes),
        out_shape=(
            jax.ShapeDtypeStruct(velocity.shape, jnp.float32),
            jax.ShapeDtypeStruct((NODES, L4), jnp.float32),
            jax.ShapeDtypeStruct((L4, L4), jnp.bfloat16),
        ),
        in_specs=[hbm] * 6,
        out_specs=(vmem, vmem, vmem),
        scratch_shapes=[
            pltpu.VMEM(velocity.shape, jnp.float32),
            pltpu.VMEM((NODES, L4), jnp.float32),
            pltpu.VMEM(projection.shape, jnp.float32),
            pltpu.VMEM((1, NV), jnp.int32),
            pltpu.VMEM(slot_element.shape, jnp.int32),
            pltpu.VMEM(element_cell.shape, jnp.int32),
            dma((6,)),
            pltpu.VMEM((3, 3, X + 2, Y, Z), jnp.float32),
            pltpu.VMEM((3, 2, 3, X, Z), jnp.float32),
            pltpu.VMEM((2, 2, 3, X, Z), jnp.float32),
            pltpu.VMEM((3, 2, Y, Z), jnp.float32),
            pltpu.VMEM((2, 2, Y, Z), jnp.float32),
            pltpu.VMEM((2, 6, FACE, L4), jnp.bfloat16),
            pltpu.VMEM((2, 6, FACE, L4), jnp.bfloat16),
            pltpu.VMEM((2, peers, cap * VS, 4 * PB), travel),
            pltpu.VMEM((2, peers, cap * VS, 4 * PB), travel),
            pltpu.VMEM((NODES, L4), jnp.float32),
            pltpu.VMEM((NODES, L4), jnp.float32),
            pltpu.VMEM((X // (2 * VS), 4 * PB, Z), jnp.float32),
            pltpu.VMEM((R, NV * 2 * VS), jnp.bfloat16),
            pltpu.VMEM((VS * E, R), jnp.bfloat16),
            pltpu.VMEM((NODES, 4 * VS**3), jnp.bfloat16),
            pltpu.VMEM((4 * PB, L4), jnp.float32),
            pltpu.VMEM((blocks * VS**3, L4), jnp.float32),
            dma((2, 6)), dma((2, 6)), dma((2, 6)), dma((2, 6)),
            dma((2, peers - 1)), dma((2, peers - 1)),
        ],
        compiler_params=pltpu.CompilerParams(
            collective_id=0, has_side_effects=True, vmem_limit_bytes=32 * 1024 * 1024
        ),
    )(
        *[
            pltpu.with_memory_space_constraint(x, pltpu.HBM)
            for x in (
                velocity, cells, projection, owner_index.reshape(1, NV), slot_element,
                element_cell,
            )
        ]
    )
    flow, stored = pl.pallas_call(
        finish,
        out_shape=(
            jax.ShapeDtypeStruct(velocity.shape, jnp.float32),
            jax.ShapeDtypeStruct((NODES, L4), jnp.float32),
        ),
        in_specs=[vmem] * 3,
        out_specs=(hbm, hbm),
        scratch_shapes=[pltpu.VMEM((NODES, L4), jnp.float32), dma((2,))],
        compiler_params=pltpu.CompilerParams(vmem_limit_bytes=16 * 1024 * 1024),
    )(flow, wave, perm)
    stored = stored.reshape(E, blocks, 4, L4).transpose(0, 2, 1, 3).reshape(acoustic.shape)
    return flow, stored


def solution(mesh):
    in_specs = (
        P(None, "gx", "gy", "gz"),
        P(("gx", "gy", "gz"), None, None),
        P(),
        P(("gx", "gy", "gz"), None),
        P(("gx", "gy", "gz"), None),
        P(("gx", "gy", "gz"), None),
    )
    out_specs = (P(None, "gx", "gy", "gz"), P(("gx", "gy", "gz"), None, None))
    return jax.shard_map(
        on_device, mesh=mesh, in_specs=in_specs, out_specs=out_specs, check_vma=False
    )
```

```python
import functools

import jax
import jax.numpy as jnp
import numpy as np
from jax import lax
from jax.experimental import pallas as pl
from jax.experimental.pallas import tpu as pltpu
from jax.sharding import PartitionSpec as P

VS = 4
ORDER = 7
EBX = 1
EBY = 2
EBZ = 16
K = ORDER + 1
FACE = K * K
NODES = K**3

HIGHEST = lax.Precision.HIGHEST
FLOW_STEP = 0.1
VISCOSITY = 0.05
WAVE_STEP = 0.02
SOURCE_GAIN = 25.0
MESH = pl.DeviceIdType.MESH


def legendre_table(points, order):
    columns = [points * 0.0 + 1.0, points]
    for degree in range(2, order + 1):
        columns.append(
            ((2 * degree - 1) * points * columns[degree - 1] - (degree - 1) * columns[degree - 2])
            / degree
        )
    return np.stack(columns, axis=1)


def lobatto_tables(order):
    point_count = order + 1
    points = -np.cos(np.pi * np.arange(point_count) / order)
    for newton_step in range(60):
        legendre = legendre_table(points, order)
        points = points - (points * legendre[:, order] - legendre[:, order - 1]) / (
            point_count * legendre[:, order]
        )
    legendre = legendre_table(points, order)
    highest = legendre[:, order]
    spacing = points[:, None] - points[None, :] + np.eye(point_count)
    derivative = highest[:, None] / (highest[None, :] * spacing)
    derivative = derivative * (1.0 - np.eye(point_count))
    derivative[0, 0] = -order * point_count / 4.0
    derivative[order, order] = order * point_count / 4.0
    return derivative


def iota(shape, axis):
    return lax.broadcasted_iota(jnp.int32, shape, axis)


def as_float(mask):
    return jnp.where(mask, 1.0, 0.0).astype(jnp.float32)


def to_column(row, count):
    eye = iota((count, count), 0) == iota((count, count), 1)
    return jnp.sum(jnp.where(eye, row, 0.0), axis=1, keepdims=True)


def spread_row(column, count, width, group):
    pick = iota((count, width), 0) == iota((count, width), 1) // group
    return jnp.sum(jnp.where(pick, column, 0.0), axis=0, keepdims=True)


def split(value):
    high = value.astype(jnp.bfloat16)
    low = (value - high.astype(jnp.float32)).astype(jnp.bfloat16)
    return high, low


def dot(a, b, contract=((1,), (0,)), precision=None):
    return lax.dot_general(
        a, b, (contract, ((), ())), preferred_element_type=jnp.float32, precision=precision
    )


def permutation(cell_row, elements):
    total = 4 * elements
    rows = iota((total, elements), 0)
    cell = jnp.sum(
        jnp.where(iota((total, elements), 1) == rows % elements, cell_row, 0.0),
        axis=1, keepdims=True,
    )
    r = iota((total, total), 0)
    goal = (r - r % elements).astype(jnp.float32) + cell
    return as_float(iota((total, total), 1).astype(jnp.float32) == goal).astype(jnp.bfloat16)


def swap(value, group, along, width):
    axis = value.ndim - 1
    total = 4 * width
    here = (1 + along) * width
    up = pltpu.roll(value, here, axis)
    down = up if 2 * here == total else pltpu.roll(value, total - here, axis)
    return jnp.where(group == 0, down, jnp.where(group == 1 + along, up, 0.0))


def derive(values, table):
    half = K // 2
    even = [values[j] + values[K - 1 - j] for j in range(half)]
    odd = [values[j] - values[K - 1 - j] for j in range(half)]
    result = [None] * K
    for a in range(half):
        first = sum(
            float(0.5 * (table[a, j] - table[a, K - 1 - j])) * odd[j] for j in range(half)
        )
        second = sum(
            float(0.5 * (table[a, j] + table[a, K - 1 - j])) * even[j] for j in range(half)
        )
        result[a] = first + second
        result[K - 1 - a] = first - second
    return result


def kernel(
    sizes,
    u_hbm, ac_hbm, proj_hbm, owner_hbm, slot_hbm, cell_hbm,
    u_out, ac_out, perm_out,
    u_in, ac_in, proj_in, owner_in, slot_in, cell_in, in_sems, flow, y_send, y_recv, z_send, z_recv, tr_send, tr_recv, vol_send, vol_recv,
    q_ref, acc, lhs, place, gather, proj_ref, summed, spare,
    v_ssem, v_rsem, t_ssem, t_rsem, p_ssem, p_rsem,
):
    nx, ny, nz, X, Y, Z, E, NV, cap = sizes
    peers = ny * nz
    gx, gy, gz = lax.axis_index("gx"), lax.axis_index("gy"), lax.axis_index("gz")
    me = gy * nz + gz
    across = [
        {"gx": lax.rem(gx + nx - 1, nx)}, {"gx": lax.rem(gx + 1, nx)},
        {"gy": lax.rem(gy + ny - 1, ny)}, {"gy": lax.rem(gy + 1, ny)},
        {"gz": lax.rem(gz + nz - 1, nz)}, {"gz": lax.rem(gz + 1, nz)},
    ]
    others = []
    for k in range(1, peers):
        p = lax.rem(me + k, peers)
        others.append((p, {"gy": lax.div(p, nz), "gz": lax.rem(p, nz)}))

    barrier = pltpu.get_barrier_semaphore()
    for target in across[:2] + [t for _, t in others]:
        pl.semaphore_signal(barrier, inc=1, device_id=target, device_id_type=MESH)

    sources = (u_hbm, owner_hbm, cell_hbm, ac_hbm, slot_hbm, proj_hbm)
    targets = (u_in, owner_in, cell_in, ac_in, slot_in, proj_in)
    loads = [
        pltpu.make_async_copy(src, dst, in_sems.at[i])
        for i, (src, dst) in enumerate(zip(sources, targets))
    ]
    for load in loads:
        load.start()

    lane = iota((Y, Z), 1)
    sub = iota((Y, Z), 0)

    def pack(t, x, values, carry):
        low, high = carry
        for c in range(3):
            at = c * X + x
            low = jnp.where(lane == at, pltpu.roll(values[c], at, 1), low)
            high = jnp.where(lane == at, pltpu.roll(values[c], at + 1, 1), high)
            y_send[t, 0, c, pl.ds(x, 1), :] = values[c][0:1]
            y_send[t, 1, c, pl.ds(x, 1), :] = values[c][Y - 1:Y]
        return low, high

    def fill(x, carry):
        values = [u_in[c, x] for c in range(3)]
        for c in range(3):
            flow[0, c, x + 1] = values[c]
        return pack(0, x, values, carry)

    blank = jnp.zeros((Y, Z), jnp.float32)

    def velocity_copies(t):
        result = []
        for f in range(6):
            s = f % 2
            if f < 2:
                src = flow.at[t, :, X if s else 1]
                dst = flow.at[t, :, 0 if s else X + 1]
            elif f < 4:
                src, dst = y_send.at[t, s], y_recv.at[t, 1 - s]
            else:
                src, dst = z_send.at[t, s], z_recv.at[t, 1 - s]
            result.append(
                pltpu.make_async_remote_copy(
                    src_ref=src, dst_ref=dst, send_sem=v_ssem.at[t, f],
                    recv_sem=v_rsem.at[t, f ^ 1], device_id=across[f], device_id_type=MESH,
                )
            )
        return result

    def trace_copies(t):
        return [
            pltpu.make_async_remote_copy(
                src_ref=tr_send.at[t, f], dst_ref=tr_recv.at[t, f ^ 1],
                send_sem=t_ssem.at[t, f], recv_sem=t_rsem.at[t, f ^ 1],
                device_id=across[f], device_id_type=MESH,
            )
            for f in range(6)
        ]

    def volume_copies(t):
        return [
            pltpu.make_async_remote_copy(
                src_ref=vol_send.at[t, p], dst_ref=vol_recv.at[t, me],
                send_sem=p_ssem.at[t, k], recv_sem=p_rsem.at[t, k],
                device_id=target, device_id_type=MESH,
            )
            for k, (p, target) in enumerate(others)
        ]

    loads[0].wait()
    low, high = lax.fori_loop(0, X, fill, (blank, blank), unroll=True)
    z_send[0, 0] = low
    z_send[0, 1] = high
    pl.semaphore_wait(barrier, peers + 1)

    def send_halos(t):
        copies = velocity_copies(t)
        for f in (0, 1, 4, 5, 2, 3):
            copies[f].start()

    send_halos(0)

    for load in loads[1:4]:
        load.wait()
    own_row = owner_in[...].astype(jnp.float32)
    own = to_column(own_row, NV)
    matches = (own == own_row) & (iota((NV, NV), 1) < iota((NV, NV), 0))
    rank = jnp.sum(as_float(matches), axis=1, keepdims=True)
    slot_of = own * float(cap) + rank
    W = NV * 2 * VS
    slot_row = spread_row(slot_of, NV, W, 2 * VS)
    wl = iota((1, W), 1)
    goal = slot_row * float(VS) + ((wl % (2 * VS)) // 2).astype(jnp.float32)
    goal = jnp.where(wl % 2 == 0, goal, -1.0)
    place[...] = as_float(
        iota((peers * cap * VS, W), 0).astype(jnp.float32) == goal
    ).astype(jnp.bfloat16)

    L4 = 4 * E
    cell_row = cell_in[...].astype(jnp.float32)
    perm = permutation(cell_row, E)
    perm_out[...] = perm
    blocks = NODES // L4
    stored = []
    for j in range(blocks):
        parts = [ac_in[pl.ds(4 * j + v, E, stride=4 * blocks), :] for v in range(4)]
        stored.append(jnp.concatenate(parts, axis=0).T)
    ah, al = split(jnp.concatenate(stored, axis=0))
    q_ref[...] = dot(
        jnp.concatenate([ah, al], axis=1), jnp.concatenate([perm, perm], axis=0)
    )

    def trace(f):
        a, s = f // 2, f % 2
        if a == 0:
            return q_ref[s * (K - 1) * FACE:s * (K - 1) * FACE + FACE, :]
        if a == 1:
            base = s * (K - 1) * K
            return jnp.concatenate(
                [q_ref[i * FACE + base:i * FACE + base + K, :] for i in range(K)], axis=0
            )
        return q_ref[pl.ds(s * (K - 1), FACE, stride=K), :]

    def send_traces(t):
        for f in range(6):
            tr_send[t, f] = trace(f).astype(jnp.bfloat16)
        for copy in trace_copies(t):
            copy.start()

    send_traces(0)

    R = peers * cap * VS
    PB = VS * Y
    cells = VS**3

    def source_tables():
        slots = peers * cap
        slot_col = to_column(slot_in[...].astype(jnp.float32), slots)
        element_row = spread_row(slot_col, slots, R, VS)
        cell_col = to_column(cell_row, E)
        target_row = jnp.sum(
            jnp.where(iota((E, R), 0).astype(jnp.float32) == element_row, cell_col, 0.0),
            axis=0, keepdims=True,
        )
        goal = target_row + ((iota((1, R), 1) % VS) * E).astype(jnp.float32)
        gather[...] = as_float(
            iota((VS * E, R), 0).astype(jnp.float32) == goal
        ).astype(jnp.bfloat16)
        blocks = NODES // L4
        for j in range(blocks):
            spare[j * cells:(j + 1) * cells, :] = proj_in[:, j * L4:(j + 1) * L4]
        rows = [
            jnp.concatenate(
                [spare[pl.ds(j * cells + c, VS * VS, stride=VS), :] for j in range(blocks)], axis=1
            )
            for c in range(VS)
        ]
        scaled = (-WAVE_STEP * SOURCE_GAIN) * jnp.concatenate(rows, axis=0)
        high, low = split(scaled)
        both = jnp.concatenate([high.astype(jnp.float32), low.astype(jnp.float32)], axis=0)
        turned = both.T.astype(jnp.bfloat16)
        proj_ref[...] = jnp.concatenate([turned, turned], axis=1)

    table = -WAVE_STEP * lobatto_tables(ORDER)
    group3 = iota((K, K, L4), 2) // E
    group2 = iota((FACE, L4), 1) // E
    sub3 = iota((K, K, L4), 1)

    def local_rates():
        factors = []
        subl = iota((K, L4), 0)
        for k in range(K):
            factor = jnp.zeros((K, L4), jnp.float32)
            for c in range(K):
                factor = jnp.where(subl == c, float(table[c, (c - k) % K]), factor)
            factors.append(factor)

        def first(i, carry):
            at = pl.multiple_of(i * FACE, FACE)
            x = q_ref[pl.ds(at, FACE), :].reshape(K, K, L4)
            total = x
            s2 = swap(x, group3, 2, E)
            for k in range(K):
                rolled = s2 if k == 0 else pltpu.roll(s2, k, 1)
                total = total + factors[k][None] * rolled
            s1 = swap(x, group3, 1, E)
            parts = derive([s1[j] for j in range(K)], table)
            total = total + jnp.stack(parts)
            acc[pl.ds(at, FACE), :] = total.reshape(FACE, L4)
            return carry

        lax.fori_loop(0, K, first, 0, unroll=True)

        def second(i, carry):
            ats = [pl.multiple_of(a * FACE + i * K, K) for a in range(K)]
            x = jnp.stack([q_ref[pl.ds(at, K), :] for at in ats])
            s0 = swap(x, group3, 0, E)
            parts = derive([s0[j] for j in range(K)], table)
            for at, part in zip(ats, parts):
                acc[pl.ds(at, K), :] += part
            return carry

        lax.fori_loop(0, K, second, 0, unroll=True)

    lane2 = iota((FACE, L4), 1)
    y_of = (lane2 % E) // EBZ
    z_of = lane2 % EBZ
    scale = WAVE_STEP * 0.5 * ORDER * (ORDER + 1) / 2.0

    def add_flux(t):
        for f in range(6):
            a, s = f // 2, f % 2
            inner = trace(f)
            other = tr_recv[t, f].astype(jnp.float32)
            if a == 0:
                outer = other
            elif a == 1:
                mine = trace(f ^ 1)
                edge = 0 if s else EBY - 1
                mixed = jnp.where(y_of == edge, other, mine)
                near = EBZ if s == 0 else L4 - EBZ
                wrap = (L4 - (EBY - 1) * EBZ) if s == 0 else (EBY - 1) * EBZ
                outer = jnp.where(
                    y_of == (EBY - 1 if s else 0),
                    pltpu.roll(mixed, wrap, 1), pltpu.roll(mixed, near, 1),
                )
            else:
                mine = trace(f ^ 1)
                edge = 0 if s else EBZ - 1
                mixed = jnp.where(z_of == edge, other, mine)
                near = 1 if s == 0 else L4 - 1
                wrap = (L4 - (EBZ - 1)) if s == 0 else EBZ - 1
                outer = jnp.where(
                    z_of == (EBZ - 1 if s else 0),
                    pltpu.roll(mixed, wrap, 1), pltpu.roll(mixed, near, 1),
                )
            jump = inner - outer
            turned = swap(jump, group2, a, E)
            flux = scale * ((turned if s else -turned) - jump)
            if a == 0:
                base = s * (K - 1) * FACE
                acc[base:base + FACE, :] += flux
            elif a == 1:
                base = s * (K - 1) * K
                for i in range(K):
                    at = i * FACE + base
                    acc[at:at + K, :] += flux[i * K:(i + 1) * K]
            else:
                where = pl.ds(s * (K - 1), FACE, stride=K)
                acc[where, :] = acc[where, :] + flux

    def flow_step(t):
        z_low = z_recv[t, 0]
        z_high = z_recv[t, 1]

        def column(x, carry):
            centre = [flow[t, c, x + 1] for c in range(3)]
            below, above = [], []
            for c in range(3):
                at = c * X + x
                u = centre[c]
                pair = (flow[t, c, x], flow[t, c, x + 2])
                y_low = y_recv[t, 0, c, pl.ds(x, 1), :]
                y_high = y_recv[t, 1, c, pl.ds(x, 1), :]
                ym = jnp.where(sub == 0, y_low, pltpu.roll(u, 1, 0))
                yp = jnp.where(sub == Y - 1, y_high, pltpu.roll(u, Y - 1, 0))
                zm = jnp.where(
                    lane == 0, pltpu.roll(z_low, lax.rem(Z - at, Z), 1), pltpu.roll(u, 1, 1)
                )
                zp = jnp.where(
                    lane == Z - 1, pltpu.roll(z_high, Z - 1 - at, 1), pltpu.roll(u, Z - 1, 1)
                )
                below.append((pair[0], ym, zm))
                above.append((pair[1], yp, zp))
            slope = [[0.5 * (above[c][a] - below[c][a]) for c in range(3)] for a in range(3)]
            updated = []
            for c in range(3):
                rate = VISCOSITY * (
                    (above[c][0] + below[c][0])
                    + (above[c][1] + below[c][1])
                    + (above[c][2] + below[c][2])
                    - 6.0 * centre[c]
                )
                for a in range(3):
                    rate = rate - centre[a] * slope[a][c]
                updated.append(centre[c] + FLOW_STEP * rate)
            w = [
                slope[1][2] - slope[2][1], slope[2][0] - slope[0][2], slope[0][1] - slope[1][0]
            ]
            lamb = [
                w[1] * centre[2] - w[2] * centre[1],
                w[2] * centre[0] - w[0] * centre[2],
                w[0] * centre[1] - w[1] * centre[0],
            ]
            for c in range(3):
                flow[t + 1, c, x + 1] = updated[c]
                u_out[c, x] = updated[c]
            carry = pack(t + 1, x, updated, carry)
            return lamb, carry

        def couple(i, carry):
            first, carry = column(2 * i, carry)
            second, carry = column(2 * i + 1, carry)
            block = lax.div(i, VS)
            row = lax.rem(i, VS)
            for c in range(3):
                total = first[c] + second[c]
                total = total + pltpu.roll(total, Y - 1, 0)
                total = total + pltpu.roll(total, Z - 1, 1)
                at = pl.multiple_of(c * PB + row * Y, Y)
                lhs[block, pl.ds(at, Y), :] = 0.125 * total
            return carry

        carry = lax.fori_loop(0, X // 2, couple, (blank, blank), unroll=True)
        z_send[t + 1, 0] = carry[0]
        z_send[t + 1, 1] = carry[1]

    def send_volumes(t):
        wide = jnp.concatenate([lhs[i] for i in range(X // (2 * VS))], axis=1)
        sent = dot(place[...], wide.astype(jnp.bfloat16), ((1,), (1,)))
        vol_send[t] = sent.astype(vol_send.dtype).reshape(peers, cap * VS, 4 * PB)
        for copy in volume_copies(t):
            copy.start()
        vol_recv[t, me] = vol_send[t, me]

    def add_source(t):
        received = vol_recv[t].reshape(R, 4 * PB).astype(jnp.bfloat16)
        summed[...] = dot(gather[...], received).T
        count = VS * VS
        group = iota((count, L4), 1) // E
        parts = [summed[pl.ds(v * PB, count, stride=2), :] for v in range(3)]
        blocks = []
        for c in range(VS):
            block = jnp.zeros((count, L4), jnp.float32)
            for v in range(3):
                shift = ((1 + v - c) * E) % L4
                part = pltpu.roll(parts[v], shift, 1) if shift else parts[v]
                block = jnp.where(group == 1 + v, part, block)
            blocks.append(block)
        high, low = split(jnp.concatenate(blocks, axis=0))
        acc[...] += dot(proj_ref[...], jnp.concatenate([high, high, low, low], axis=0))

    lhs[...] = jnp.zeros_like(lhs)

    def arrive(copies):
        for copy in copies:
            copy.wait_recv()

    def flow_part(k, carry):
        arrive(velocity_copies(k))
        flow_step(k)

        @pl.when(k == 0)
        def _():
            send_halos(1)

        send_volumes(k)
        return carry

    def step(t, carry):
        local_rates()

        @pl.when(t == 0)
        def _():
            lax.fori_loop(0, 2, flow_part, 0)

        @pl.when(t == 1)
        def _():
            arrive(volume_copies(1))
            add_source(1)

        arrive(trace_copies(t))
        add_flux(t)

        @pl.when(t == 0)
        def _():
            arrive(volume_copies(0))
            add_source(0)
            q_ref[...] = acc[...]
            send_traces(1)

        return carry

    for load in loads[4:]:
        load.wait()
    source_tables()
    lax.fori_loop(0, 2, step, 0)
    ac_out[...] = acc[...]

    def leave(t, carry):
        for copies in (velocity_copies(t), trace_copies(t), volume_copies(t)):
            for copy in copies:
                copy.wait_send()
        return carry

    lax.fori_loop(0, 2, leave, 0)


def finish(u_in, q_in, perm_in, u_hbm, ac_hbm, ac_out, sems):
    flow_copy = pltpu.make_async_copy(u_in, u_hbm, sems.at[0])
    flow_copy.start()
    nodes, total = q_in.shape
    E = total // 4
    perm = perm_in[...]
    high, low = split(q_in[...])
    stored = dot(
        jnp.concatenate([perm, perm], axis=1), jnp.concatenate([high, low], axis=1), ((1,), (1,))
    )
    blocks = nodes // total
    for j in range(blocks):
        for v in range(4):
            ac_out[pl.ds(4 * j + v, E, stride=4 * blocks), :] = stored[
                v * E:(v + 1) * E, j * total:(j + 1) * total
            ]
    wave_copy = pltpu.make_async_copy(ac_out, ac_hbm, sems.at[1])
    wave_copy.start()
    flow_copy.wait()
    wave_copy.wait()


def on_device(velocity, acoustic, projection, owner_index, slot_element, element_cell):
    nx, ny, nz = lax.axis_size("gx"), lax.axis_size("gy"), lax.axis_size("gz")
    _, X, Y, Z = velocity.shape
    E = acoustic.shape[0]
    NV = owner_index.shape[0]
    peers = ny * nz
    cap = slot_element.shape[1] // peers
    sizes = (nx, ny, nz, X, Y, Z, E, NV, cap)
    R = peers * cap * VS
    PB = VS * Y
    L4 = 4 * E
    blocks = NODES // L4
    travel = jnp.bfloat16 if (cap * VS) % 16 == 0 else jnp.float32
    vmem = pl.BlockSpec(memory_space=pltpu.VMEM)
    hbm = pl.BlockSpec(memory_space=pltpu.HBM)
    dma = pltpu.SemaphoreType.DMA
    cells = acoustic.reshape(E, 4, blocks, L4).transpose(0, 2, 1, 3).reshape(NODES, L4)
    flow, wave, perm = pl.pallas_call(
        functools.partial(kernel, sizes),
        out_shape=(
            jax.ShapeDtypeStruct(velocity.shape, jnp.float32),
            jax.ShapeDtypeStruct((NODES, L4), jnp.float32),
            jax.ShapeDtypeStruct((L4, L4), jnp.bfloat16),
        ),
        in_specs=[hbm] * 6,
        out_specs=(vmem, vmem, vmem),
        scratch_shapes=[
            pltpu.VMEM(velocity.shape, jnp.float32),
            pltpu.VMEM((NODES, L4), jnp.float32),
            pltpu.VMEM(projection.shape, jnp.float32),
            pltpu.VMEM((1, NV), jnp.int32),
            pltpu.VMEM(slot_element.shape, jnp.int32),
            pltpu.VMEM(element_cell.shape, jnp.int32),
            dma((6,)),
            pltpu.VMEM((3, 3, X + 2, Y, Z), jnp.float32),
            pltpu.VMEM((3, 2, 3, X, Z), jnp.float32),
            pltpu.VMEM((2, 2, 3, X, Z), jnp.float32),
            pltpu.VMEM((3, 2, Y, Z), jnp.float32),
            pltpu.VMEM((2, 2, Y, Z), jnp.float32),
            pltpu.VMEM((2, 6, FACE, L4), jnp.bfloat16),
            pltpu.VMEM((2, 6, FACE, L4), jnp.bfloat16),
            pltpu.VMEM((2, peers, cap * VS, 4 * PB), travel),
            pltpu.VMEM((2, peers, cap * VS, 4 * PB), travel),
            pltpu.VMEM((NODES, L4), jnp.float32),
            pltpu.VMEM((NODES, L4), jnp.float32),
            pltpu.VMEM((X // (2 * VS), 4 * PB, Z), jnp.float32),
            pltpu.VMEM((R, NV * 2 * VS), jnp.bfloat16),
            pltpu.VMEM((VS * E, R), jnp.bfloat16),
            pltpu.VMEM((NODES, 4 * VS**3), jnp.bfloat16),
            pltpu.VMEM((4 * PB, L4), jnp.float32),
            pltpu.VMEM((blocks * VS**3, L4), jnp.float32),
            dma((2, 6)), dma((2, 6)), dma((2, 6)), dma((2, 6)),
            dma((2, peers - 1)), dma((2, peers - 1)),
        ],
        compiler_params=pltpu.CompilerParams(
            collective_id=0, has_side_effects=True, vmem_limit_bytes=32 * 1024 * 1024
        ),
    )(
        *[
            pltpu.with_memory_space_constraint(x, pltpu.HBM)
            for x in (
                velocity, cells, projection, owner_index.reshape(1, NV), slot_element,
                element_cell,
            )
        ]
    )
    flow, stored = pl.pallas_call(
        finish,
        out_shape=(
            jax.ShapeDtypeStruct(velocity.shape, jnp.float32),
            jax.ShapeDtypeStruct((NODES, L4), jnp.float32),
        ),
        in_specs=[vmem] * 3,
        out_specs=(hbm, hbm),
        scratch_shapes=[pltpu.VMEM((NODES, L4), jnp.float32), dma((2,))],
        compiler_params=pltpu.CompilerParams(vmem_limit_bytes=16 * 1024 * 1024),
    )(flow, wave, perm)
    stored = stored.reshape(E, blocks, 4, L4).transpose(0, 2, 1, 3).reshape(acoustic.shape)
    return flow, stored


def solution(mesh):
    in_specs = (
        P(None, "gx", "gy", "gz"),
        P(("gx", "gy", "gz"), None, None),
        P(),
        P(("gx", "gy", "gz"), None),
        P(("gx", "gy", "gz"), None),
        P(("gx", "gy", "gz"), None),
    )
    out_specs = (P(None, "gx", "gy", "gz"), P(("gx", "gy", "gz"), None, None))
    return jax.shard_map(
        on_device, mesh=mesh, in_specs=in_specs, out_specs=out_specs, check_vma=False
    )
```

```python
import functools

import jax
import jax.numpy as jnp
import numpy as np
from jax import lax
from jax.experimental import pallas as pl
from jax.experimental.pallas import tpu as pltpu
from jax.sharding import PartitionSpec as P

VS = 4
ORDER = 7
EBX = 1
EBY = 2
EBZ = 16
K = ORDER + 1
FACE = K * K
NODES = K**3

HIGHEST = lax.Precision.HIGHEST
FLOW_STEP = 0.1
VISCOSITY = 0.05
WAVE_STEP = 0.02
SOURCE_GAIN = 25.0
MESH = pl.DeviceIdType.MESH


def legendre_table(points, order):
    columns = [points * 0.0 + 1.0, points]
    for degree in range(2, order + 1):
        columns.append(
            ((2 * degree - 1) * points * columns[degree - 1] - (degree - 1) * columns[degree - 2])
            / degree
        )
    return np.stack(columns, axis=1)


def lobatto_tables(order):
    point_count = order + 1
    points = -np.cos(np.pi * np.arange(point_count) / order)
    for newton_step in range(60):
        legendre = legendre_table(points, order)
        points = points - (points * legendre[:, order] - legendre[:, order - 1]) / (
            point_count * legendre[:, order]
        )
    legendre = legendre_table(points, order)
    highest = legendre[:, order]
    spacing = points[:, None] - points[None, :] + np.eye(point_count)
    derivative = highest[:, None] / (highest[None, :] * spacing)
    derivative = derivative * (1.0 - np.eye(point_count))
    derivative[0, 0] = -order * point_count / 4.0
    derivative[order, order] = order * point_count / 4.0
    return derivative


def iota(shape, axis):
    return lax.broadcasted_iota(jnp.int32, shape, axis)


def as_float(mask):
    return jnp.where(mask, 1.0, 0.0).astype(jnp.float32)


def to_column(row, count):
    eye = iota((count, count), 0) == iota((count, count), 1)
    return jnp.sum(jnp.where(eye, row, 0.0), axis=1, keepdims=True)


def spread_row(column, count, width, group):
    pick = iota((count, width), 0) == iota((count, width), 1) // group
    return jnp.sum(jnp.where(pick, column, 0.0), axis=0, keepdims=True)


def split(value):
    high = value.astype(jnp.bfloat16)
    low = (value - high.astype(jnp.float32)).astype(jnp.bfloat16)
    return high, low


def dot(a, b, contract=((1,), (0,)), precision=None):
    return lax.dot_general(
        a, b, (contract, ((), ())), preferred_element_type=jnp.float32, precision=precision
    )


def permutation(cell_row, elements):
    total = 4 * elements
    rows = iota((total, elements), 0)
    cell = jnp.sum(
        jnp.where(iota((total, elements), 1) == rows % elements, cell_row, 0.0),
        axis=1, keepdims=True,
    )
    r = iota((total, total), 0)
    goal = (r - r % elements).astype(jnp.float32) + cell
    return as_float(iota((total, total), 1).astype(jnp.float32) == goal).astype(jnp.bfloat16)


def swap(value, group, along, width):
    axis = value.ndim - 1
    total = 4 * width
    here = (1 + along) * width
    up = pltpu.roll(value, here, axis)
    down = up if 2 * here == total else pltpu.roll(value, total - here, axis)
    return jnp.where(group == 0, down, jnp.where(group == 1 + along, up, 0.0))


def derive(values, table):
    half = K // 2
    even = [values[j] + values[K - 1 - j] for j in range(half)]
    odd = [values[j] - values[K - 1 - j] for j in range(half)]
    result = [None] * K
    for a in range(half):
        first = sum(
            float(0.5 * (table[a, j] - table[a, K - 1 - j])) * odd[j] for j in range(half)
        )
        second = sum(
            float(0.5 * (table[a, j] + table[a, K - 1 - j])) * even[j] for j in range(half)
        )
        result[a] = first + second
        result[K - 1 - a] = first - second
    return result


def kernel(
    sizes,
    u_hbm, ac_hbm, proj_hbm, owner_hbm, slot_hbm, cell_hbm,
    u_out, ac_out, perm_out,
    u_in, ac_in, proj_in, owner_in, slot_in, cell_in, in_sems, flow, y_send, y_recv, z_send, z_recv, tr_send, tr_recv, vol_send, vol_recv,
    q_ref, acc, lhs, place, gather, proj_ref, summed, spare,
    v_ssem, v_rsem, t_ssem, t_rsem, p_ssem, p_rsem,
):
    nx, ny, nz, X, Y, Z, E, NV, cap = sizes
    peers = ny * nz
    gx, gy, gz = lax.axis_index("gx"), lax.axis_index("gy"), lax.axis_index("gz")
    me = gy * nz + gz
    across = [
        {"gx": lax.rem(gx + nx - 1, nx)}, {"gx": lax.rem(gx + 1, nx)},
        {"gy": lax.rem(gy + ny - 1, ny)}, {"gy": lax.rem(gy + 1, ny)},
        {"gz": lax.rem(gz + nz - 1, nz)}, {"gz": lax.rem(gz + 1, nz)},
    ]
    others = []
    for k in range(1, peers):
        p = lax.rem(me + k, peers)
        others.append((p, {"gy": lax.div(p, nz), "gz": lax.rem(p, nz)}))

    barrier = pltpu.get_barrier_semaphore()
    for target in across[:2] + [t for _, t in others]:
        pl.semaphore_signal(barrier, inc=1, device_id=target, device_id_type=MESH)

    sources = (u_hbm, cell_hbm, ac_hbm, owner_hbm, slot_hbm, proj_hbm)
    targets = (u_in, cell_in, ac_in, owner_in, slot_in, proj_in)
    loads = [
        pltpu.make_async_copy(src, dst, in_sems.at[i])
        for i, (src, dst) in enumerate(zip(sources, targets))
    ]
    for load in loads:
        load.start()

    lane = iota((Y, Z), 1)
    sub = iota((Y, Z), 0)

    def pack(t, x, values, carry):
        low, high = carry
        for c in range(3):
            at = c * X + x
            low = jnp.where(lane == at, pltpu.roll(values[c], at, 1), low)
            high = jnp.where(lane == at, pltpu.roll(values[c], at + 1, 1), high)
            y_send[t, 0, c, pl.ds(x, 1), :] = values[c][0:1]
            y_send[t, 1, c, pl.ds(x, 1), :] = values[c][Y - 1:Y]
        return low, high

    def fill(x, carry):
        values = [u_in[c, x] for c in range(3)]
        for c in range(3):
            flow[0, c, x + 1] = values[c]
        return pack(0, x, values, carry)

    blank = jnp.zeros((Y, Z), jnp.float32)

    def velocity_copies(t):
        result = []
        for f in range(6):
            s = f % 2
            if f < 2:
                src = flow.at[t, :, X if s else 1]
                dst = flow.at[t, :, 0 if s else X + 1]
            elif f < 4:
                src, dst = y_send.at[t, s], y_recv.at[t, 1 - s]
            else:
                src, dst = z_send.at[t, s], z_recv.at[t, 1 - s]
            result.append(
                pltpu.make_async_remote_copy(
                    src_ref=src, dst_ref=dst, send_sem=v_ssem.at[t, f],
                    recv_sem=v_rsem.at[t, f ^ 1], device_id=across[f], device_id_type=MESH,
                )
            )
        return result

    def trace_copies(t):
        return [
            pltpu.make_async_remote_copy(
                src_ref=tr_send.at[t, f], dst_ref=tr_recv.at[t, f ^ 1],
                send_sem=t_ssem.at[t, f], recv_sem=t_rsem.at[t, f ^ 1],
                device_id=across[f], device_id_type=MESH,
            )
            for f in range(6)
        ]

    def volume_copies(t):
        return [
            pltpu.make_async_remote_copy(
                src_ref=vol_send.at[t, p], dst_ref=vol_recv.at[t, me],
                send_sem=p_ssem.at[t, k], recv_sem=p_rsem.at[t, k],
                device_id=target, device_id_type=MESH,
            )
            for k, (p, target) in enumerate(others)
        ]

    loads[0].wait()
    low, high = lax.fori_loop(0, X, fill, (blank, blank), unroll=True)
    z_send[0, 0] = low
    z_send[0, 1] = high
    pl.semaphore_wait(barrier, peers + 1)

    def send_halos(t):
        copies = velocity_copies(t)
        for f in (0, 1, 4, 5, 2, 3):
            copies[f].start()

    send_halos(0)

    L4 = 4 * E
    loads[1].wait()
    loads[2].wait()
    cell_row = cell_in[...].astype(jnp.float32)
    perm = permutation(cell_row, E)
    perm_out[...] = perm
    blocks = NODES // L4
    stored = []
    for j in range(blocks):
        parts = [ac_in[pl.ds(4 * j + v, E, stride=4 * blocks), :] for v in range(4)]
        stored.append(jnp.concatenate(parts, axis=0).T)
    ah, al = split(jnp.concatenate(stored, axis=0))
    q_ref[...] = dot(
        jnp.concatenate([ah, al], axis=1), jnp.concatenate([perm, perm], axis=0)
    )

    def trace(f):
        a, s = f // 2, f % 2
        if a == 0:
            return q_ref[s * (K - 1) * FACE:s * (K - 1) * FACE + FACE, :]
        if a == 1:
            base = s * (K - 1) * K
            return jnp.concatenate(
                [q_ref[i * FACE + base:i * FACE + base + K, :] for i in range(K)], axis=0
            )
        return q_ref[pl.ds(s * (K - 1), FACE, stride=K), :]

    def send_traces(t):
        for f in range(6):
            tr_send[t, f] = trace(f).astype(jnp.bfloat16)
        for copy in trace_copies(t):
            copy.start()

    send_traces(0)

    cells = VS**3
    for load in loads[3:]:
        load.wait()
    own_row = owner_in[...].astype(jnp.float32)
    own = to_column(own_row, NV)
    matches = (own == own_row) & (iota((NV, NV), 1) < iota((NV, NV), 0))
    rank = jnp.sum(as_float(matches), axis=1, keepdims=True)
    slot_of = own * float(cap) + rank
    W = NV * 2 * VS
    R = peers * cap * VS
    slot_row = spread_row(slot_of, NV, W, 2 * VS)
    wl = iota((1, W), 1)
    goal = slot_row * float(VS) + ((wl % (2 * VS)) // 2).astype(jnp.float32)
    goal = jnp.where(wl % 2 == 0, goal, -1.0)
    place[...] = as_float(iota((R, W), 0).astype(jnp.float32) == goal).astype(jnp.bfloat16)

    slots = peers * cap
    slot_col = to_column(slot_in[...].astype(jnp.float32), slots)
    element_row = spread_row(slot_col, slots, R, VS)
    cell_col = to_column(cell_row, E)
    target_row = jnp.sum(
        jnp.where(iota((E, R), 0).astype(jnp.float32) == element_row, cell_col, 0.0),
        axis=0, keepdims=True,
    )
    goal = target_row + ((iota((1, R), 1) % VS) * E).astype(jnp.float32)
    gather[...] = as_float(iota((VS * E, R), 0).astype(jnp.float32) == goal).astype(jnp.bfloat16)

    PB = VS * Y
    blocks = NODES // L4
    for j in range(blocks):
        spare[j * cells:(j + 1) * cells, :] = proj_in[:, j * L4:(j + 1) * L4]
    rows = [
        jnp.concatenate(
            [spare[pl.ds(j * cells + c, VS * VS, stride=VS), :] for j in range(blocks)], axis=1
        )
        for c in range(VS)
    ]
    scaled = (-WAVE_STEP * SOURCE_GAIN) * jnp.concatenate(rows, axis=0)
    high, low = split(scaled)
    both = jnp.concatenate([high.astype(jnp.float32), low.astype(jnp.float32)], axis=0)
    turned = both.T.astype(jnp.bfloat16)
    proj_ref[...] = jnp.concatenate([turned, turned], axis=1)

    table = -WAVE_STEP * lobatto_tables(ORDER)
    group3 = iota((K, K, L4), 2) // E
    group2 = iota((FACE, L4), 1) // E
    sub3 = iota((K, K, L4), 1)

    def local_rates():
        factors = []
        subl = iota((K, L4), 0)
        for k in range(K):
            factor = jnp.zeros((K, L4), jnp.float32)
            for c in range(K):
                factor = jnp.where(subl == c, float(table[c, (c - k) % K]), factor)
            factors.append(factor)

        def first(i, carry):
            at = pl.multiple_of(i * FACE, FACE)
            x = q_ref[pl.ds(at, FACE), :].reshape(K, K, L4)
            total = x
            s2 = swap(x, group3, 2, E)
            for k in range(K):
                rolled = s2 if k == 0 else pltpu.roll(s2, k, 1)
                total = total + factors[k][None] * rolled
            s1 = swap(x, group3, 1, E)
            parts = derive([s1[j] for j in range(K)], table)
            total = total + jnp.stack(parts)
            acc[pl.ds(at, FACE), :] = total.reshape(FACE, L4)
            return carry

        lax.fori_loop(0, K, first, 0, unroll=True)

        def second(i, carry):
            ats = [pl.multiple_of(a * FACE + i * K, K) for a in range(K)]
            x = jnp.stack([q_ref[pl.ds(at, K), :] for at in ats])
            s0 = swap(x, group3, 0, E)
            parts = derive([s0[j] for j in range(K)], table)
            for at, part in zip(ats, parts):
                acc[pl.ds(at, K), :] += part
            return carry

        lax.fori_loop(0, K, second, 0, unroll=True)

    lane2 = iota((FACE, L4), 1)
    y_of = (lane2 % E) // EBZ
    z_of = lane2 % EBZ
    scale = WAVE_STEP * 0.5 * ORDER * (ORDER + 1) / 2.0

    def add_flux(t):
        for f in range(6):
            a, s = f // 2, f % 2
            inner = trace(f)
            other = tr_recv[t, f].astype(jnp.float32)
            if a == 0:
                outer = other
            elif a == 1:
                mine = trace(f ^ 1)
                edge = 0 if s else EBY - 1
                mixed = jnp.where(y_of == edge, other, mine)
                near = EBZ if s == 0 else L4 - EBZ
                wrap = (L4 - (EBY - 1) * EBZ) if s == 0 else (EBY - 1) * EBZ
                outer = jnp.where(
                    y_of == (EBY - 1 if s else 0),
                    pltpu.roll(mixed, wrap, 1), pltpu.roll(mixed, near, 1),
                )
            else:
                mine = trace(f ^ 1)
                edge = 0 if s else EBZ - 1
                mixed = jnp.where(z_of == edge, other, mine)
                near = 1 if s == 0 else L4 - 1
                wrap = (L4 - (EBZ - 1)) if s == 0 else EBZ - 1
                outer = jnp.where(
                    z_of == (EBZ - 1 if s else 0),
                    pltpu.roll(mixed, wrap, 1), pltpu.roll(mixed, near, 1),
                )
            jump = inner - outer
            turned = swap(jump, group2, a, E)
            flux = scale * ((turned if s else -turned) - jump)
            if a == 0:
                base = s * (K - 1) * FACE
                acc[base:base + FACE, :] += flux
            elif a == 1:
                base = s * (K - 1) * K
                for i in range(K):
                    at = i * FACE + base
                    acc[at:at + K, :] += flux[i * K:(i + 1) * K]
            else:
                where = pl.ds(s * (K - 1), FACE, stride=K)
                acc[where, :] = acc[where, :] + flux

    def flow_step(t):
        z_low = z_recv[t, 0]
        z_high = z_recv[t, 1]

        def column(x, carry):
            centre = [flow[t, c, x + 1] for c in range(3)]
            below, above = [], []
            for c in range(3):
                at = c * X + x
                u = centre[c]
                pair = (flow[t, c, x], flow[t, c, x + 2])
                y_low = y_recv[t, 0, c, pl.ds(x, 1), :]
                y_high = y_recv[t, 1, c, pl.ds(x, 1), :]
                ym = jnp.where(sub == 0, y_low, pltpu.roll(u, 1, 0))
                yp = jnp.where(sub == Y - 1, y_high, pltpu.roll(u, Y - 1, 0))
                zm = jnp.where(
                    lane == 0, pltpu.roll(z_low, lax.rem(Z - at, Z), 1), pltpu.roll(u, 1, 1)
                )
                zp = jnp.where(
                    lane == Z - 1, pltpu.roll(z_high, Z - 1 - at, 1), pltpu.roll(u, Z - 1, 1)
                )
                below.append((pair[0], ym, zm))
                above.append((pair[1], yp, zp))
            slope = [[0.5 * (above[c][a] - below[c][a]) for c in range(3)] for a in range(3)]
            updated = []
            for c in range(3):
                rate = VISCOSITY * (
                    (above[c][0] + below[c][0])
                    + (above[c][1] + below[c][1])
                    + (above[c][2] + below[c][2])
                    - 6.0 * centre[c]
                )
                for a in range(3):
                    rate = rate - centre[a] * slope[a][c]
                updated.append(centre[c] + FLOW_STEP * rate)
            w = [
                slope[1][2] - slope[2][1], slope[2][0] - slope[0][2], slope[0][1] - slope[1][0]
            ]
            lamb = [
                w[1] * centre[2] - w[2] * centre[1],
                w[2] * centre[0] - w[0] * centre[2],
                w[0] * centre[1] - w[1] * centre[0],
            ]
            for c in range(3):
                flow[t + 1, c, x + 1] = updated[c]
                u_out[c, x] = updated[c]
            carry = pack(t + 1, x, updated, carry)
            return lamb, carry

        def couple(i, carry):
            first, carry = column(2 * i, carry)
            second, carry = column(2 * i + 1, carry)
            block = lax.div(i, VS)
            row = lax.rem(i, VS)
            for c in range(3):
                total = first[c] + second[c]
                total = total + pltpu.roll(total, Y - 1, 0)
                total = total + pltpu.roll(total, Z - 1, 1)
                at = pl.multiple_of(c * PB + row * Y, Y)
                lhs[block, pl.ds(at, Y), :] = 0.125 * total
            return carry

        carry = lax.fori_loop(0, X // 2, couple, (blank, blank), unroll=True)
        z_send[t + 1, 0] = carry[0]
        z_send[t + 1, 1] = carry[1]

    def send_volumes(t):
        wide = jnp.concatenate([lhs[i] for i in range(X // (2 * VS))], axis=1)
        sent = dot(place[...], wide.astype(jnp.bfloat16), ((1,), (1,)))
        vol_send[t] = sent.astype(vol_send.dtype).reshape(peers, cap * VS, 4 * PB)
        for copy in volume_copies(t):
            copy.start()
        vol_recv[t, me] = vol_send[t, me]

    def add_source(t):
        received = vol_recv[t].reshape(R, 4 * PB).astype(jnp.bfloat16)
        summed[...] = dot(gather[...], received).T
        count = VS * VS
        group = iota((count, L4), 1) // E
        parts = [summed[pl.ds(v * PB, count, stride=2), :] for v in range(3)]
        blocks = []
        for c in range(VS):
            block = jnp.zeros((count, L4), jnp.float32)
            for v in range(3):
                shift = ((1 + v - c) * E) % L4
                part = pltpu.roll(parts[v], shift, 1) if shift else parts[v]
                block = jnp.where(group == 1 + v, part, block)
            blocks.append(block)
        high, low = split(jnp.concatenate(blocks, axis=0))
        acc[...] += dot(proj_ref[...], jnp.concatenate([high, high, low, low], axis=0))

    lhs[...] = jnp.zeros_like(lhs)

    def arrive(copies):
        for copy in copies:
            copy.wait_recv()

    def step(t, carry):
        arrive(velocity_copies(t))
        flow_step(t)
        send_volumes(t)

        @pl.when(t == 0)
        def _():
            send_halos(1)

        @pl.when(t == 1)
        def _():
            arrive(volume_copies(0))
            add_source(0)
            q_ref[...] = acc[...]
            send_traces(1)

        local_rates()

        @pl.when(t == 1)
        def _():
            arrive(volume_copies(1))
            add_source(1)

        arrive(trace_copies(t))
        add_flux(t)
        return carry

    lax.fori_loop(0, 2, step, 0)
    ac_out[...] = acc[...]

    def leave(t, carry):
        for copies in (velocity_copies(t), trace_copies(t), volume_copies(t)):
            for copy in copies:
                copy.wait_send()
        return carry

    lax.fori_loop(0, 2, leave, 0)


def finish(u_in, q_in, perm_in, u_hbm, ac_hbm, ac_out, sems):
    flow_copy = pltpu.make_async_copy(u_in, u_hbm, sems.at[0])
    flow_copy.start()
    nodes, total = q_in.shape
    E = total // 4
    perm = perm_in[...]
    high, low = split(q_in[...])
    stored = dot(
        jnp.concatenate([perm, perm], axis=1), jnp.concatenate([high, low], axis=1), ((1,), (1,))
    )
    blocks = nodes // total
    for j in range(blocks):
        for v in range(4):
            ac_out[pl.ds(4 * j + v, E, stride=4 * blocks), :] = stored[
                v * E:(v + 1) * E, j * total:(j + 1) * total
            ]
    wave_copy = pltpu.make_async_copy(ac_out, ac_hbm, sems.at[1])
    wave_copy.start()
    flow_copy.wait()
    wave_copy.wait()


def on_device(velocity, acoustic, projection, owner_index, slot_element, element_cell):
    nx, ny, nz = lax.axis_size("gx"), lax.axis_size("gy"), lax.axis_size("gz")
    _, X, Y, Z = velocity.shape
    E = acoustic.shape[0]
    NV = owner_index.shape[0]
    peers = ny * nz
    cap = slot_element.shape[1] // peers
    sizes = (nx, ny, nz, X, Y, Z, E, NV, cap)
    R = peers * cap * VS
    PB = VS * Y
    L4 = 4 * E
    blocks = NODES // L4
    travel = jnp.bfloat16 if (cap * VS) % 16 == 0 else jnp.float32
    vmem = pl.BlockSpec(memory_space=pltpu.VMEM)
    hbm = pl.BlockSpec(memory_space=pltpu.HBM)
    dma = pltpu.SemaphoreType.DMA
    cells = acoustic.reshape(E, 4, blocks, L4).transpose(0, 2, 1, 3).reshape(NODES, L4)
    flow, wave, perm = pl.pallas_call(
        functools.partial(kernel, sizes),
        out_shape=(
            jax.ShapeDtypeStruct(velocity.shape, jnp.float32),
            jax.ShapeDtypeStruct((NODES, L4), jnp.float32),
            jax.ShapeDtypeStruct((L4, L4), jnp.bfloat16),
        ),
        in_specs=[hbm] * 6,
        out_specs=(vmem, vmem, vmem),
        scratch_shapes=[
            pltpu.VMEM(velocity.shape, jnp.float32),
            pltpu.VMEM((NODES, L4), jnp.float32),
            pltpu.VMEM(projection.shape, jnp.float32),
            pltpu.VMEM((1, NV), jnp.int32),
            pltpu.VMEM(slot_element.shape, jnp.int32),
            pltpu.VMEM(element_cell.shape, jnp.int32),
            dma((6,)),
            pltpu.VMEM((3, 3, X + 2, Y, Z), jnp.float32),
            pltpu.VMEM((3, 2, 3, X, Z), jnp.float32),
            pltpu.VMEM((2, 2, 3, X, Z), jnp.float32),
            pltpu.VMEM((3, 2, Y, Z), jnp.float32),
            pltpu.VMEM((2, 2, Y, Z), jnp.float32),
            pltpu.VMEM((2, 6, FACE, L4), jnp.bfloat16),
            pltpu.VMEM((2, 6, FACE, L4), jnp.bfloat16),
            pltpu.VMEM((2, peers, cap * VS, 4 * PB), travel),
            pltpu.VMEM((2, peers, cap * VS, 4 * PB), travel),
            pltpu.VMEM((NODES, L4), jnp.float32),
            pltpu.VMEM((NODES, L4), jnp.float32),
            pltpu.VMEM((X // (2 * VS), 4 * PB, Z), jnp.float32),
            pltpu.VMEM((R, NV * 2 * VS), jnp.bfloat16),
            pltpu.VMEM((VS * E, R), jnp.bfloat16),
            pltpu.VMEM((NODES, 4 * VS**3), jnp.bfloat16),
            pltpu.VMEM((4 * PB, L4), jnp.float32),
            pltpu.VMEM((blocks * VS**3, L4), jnp.float32),
            dma((2, 6)), dma((2, 6)), dma((2, 6)), dma((2, 6)),
            dma((2, peers - 1)), dma((2, peers - 1)),
        ],
        compiler_params=pltpu.CompilerParams(
            collective_id=0, has_side_effects=True, vmem_limit_bytes=32 * 1024 * 1024
        ),
    )(
        *[
            pltpu.with_memory_space_constraint(x, pltpu.HBM)
            for x in (
                velocity, cells, projection, owner_index.reshape(1, NV), slot_element,
                element_cell,
            )
        ]
    )
    flow, stored = pl.pallas_call(
        finish,
        out_shape=(
            jax.ShapeDtypeStruct(velocity.shape, jnp.float32),
            jax.ShapeDtypeStruct((NODES, L4), jnp.float32),
        ),
        in_specs=[vmem] * 3,
        out_specs=(hbm, hbm),
        scratch_shapes=[pltpu.VMEM((NODES, L4), jnp.float32), dma((2,))],
        compiler_params=pltpu.CompilerParams(vmem_limit_bytes=16 * 1024 * 1024),
    )(flow, wave, perm)
    stored = stored.reshape(E, blocks, 4, L4).transpose(0, 2, 1, 3).reshape(acoustic.shape)
    return flow, stored


def solution(mesh):
    in_specs = (
        P(None, "gx", "gy", "gz"),
        P(("gx", "gy", "gz"), None, None),
        P(),
        P(("gx", "gy", "gz"), None),
        P(("gx", "gy", "gz"), None),
        P(("gx", "gy", "gz"), None),
    )
    out_specs = (P(None, "gx", "gy", "gz"), P(("gx", "gy", "gz"), None, None))
    return jax.shard_map(
        on_device, mesh=mesh, in_specs=in_specs, out_specs=out_specs, check_vma=False
    )
```
